256 devices in a mesh: doc: 4 (over x), ctx: 64 (over z, y, core).
Axes of the slice: x: 4, y: 4, z: 8, core: 2. Of those that a mesh axis runs over, the one named last changes fastest.
Arguments:
- query_vectors: bfloat16 [32768, 1024], P(('doc', 'ctx')), parts along dimension 0, may hold values from -8 to 8
- key_vectors: bfloat16 [32768, 1024], P(('doc', 'ctx')), parts along dimension 0, may hold values from -8 to 8
- value_vectors: bfloat16 [32768, 1024], P(('doc', 'ctx')), parts along dimension 0, may hold values from -8 to 8
Outputs:
- attended: bfloat16 [32768, 1024], P(('doc', 'ctx')), parts along dimension 0
The draws below stay inside these ranges and needn't reach their ends.
There are 4 independent parts, one for each index of `doc`. The reference program is written for one: setup_inputs(seed, part) draws one part's arguments, and reference() takes and returns one part's arrays. A program takes and returns all parts, laid end to end along the dimension named above; each array names one. Nothing has to cross between parts.
All inputs are finite; a program needn't handle non-finite values.
Results may differ from the reference program's by a relative error of at most 0.0087.
The reference program's roundings to bfloat16 on the way count: a program that leaves them out, or rounds other values in their place, can miss the bound.
Values may be sent and summed in bfloat16 or wider, within the bound.
A program may use at most 64 MiB of HBM per device.

```python
import jax
import jax.numpy as jnp
from jax import lax

HEADS = 8
D = 1024
BLOCK = 128
TOKENS = 8192


def draw_query_vectors(key, part):
    key = jax.random.fold_in(key, 1)
    values = jnp.clip(1.8 * jax.random.normal(key, (TOKENS, D), jnp.float32), -8.0, 8.0)
    return values.astype(jnp.bfloat16)


def draw_key_vectors(key, part):
    key = jax.random.fold_in(key, 2)
    values = jnp.clip(1.8 * jax.random.normal(key, (TOKENS, D), jnp.float32), -8.0, 8.0)
    return values.astype(jnp.bfloat16)


def draw_value_vectors(key, part):
    key = jax.random.fold_in(key, 3)
    base_key, offset_key = jax.random.split(key)
    values = jax.random.normal(base_key, (TOKENS, D), jnp.float32)
    for scale_step in range((TOKENS // BLOCK).bit_length() - 1):
        extent = BLOCK << scale_step
        offset_draw = 0.5 * jax.random.normal(jax.random.fold_in(offset_key, scale_step), (TOKENS // extent, D), jnp.float32)
        values = values + jnp.repeat(offset_draw, extent, axis=0)
    return jnp.clip(values, -8.0, 8.0).astype(jnp.bfloat16)


def setup_inputs(seed: int = 0, part: int = 0) -> dict:
    seeds = jax.random.split(jax.random.key(seed), 4)
    own_keys = jax.random.split(jax.random.fold_in(seeds[3], part), 4)
    query_vectors = draw_query_vectors(jax.random.fold_in(jax.random.fold_in(seeds[3], part), 71), part)
    key_vectors = draw_key_vectors(jax.random.fold_in(jax.random.fold_in(seeds[3], part), 71), part)
    value_vectors = draw_value_vectors(jax.random.fold_in(jax.random.fold_in(seeds[3], part), 71), part)
    return dict(query_vectors=query_vectors, key_vectors=key_vectors, value_vectors=value_vectors)


masked_score = -1e30


def halve(rows):
    shape = rows.shape
    paired = rows.astype(jnp.float32).reshape(shape[:-2] + (shape[-2] // 2, 2, shape[-1]))
    return ((paired[..., 0, :] + paired[..., 1, :]) * 0.5).astype(jnp.bfloat16)


def attend(query_box, key_box, value_box, allowed, weight):
    boxes, query_count, width = query_box.shape
    key_count = key_box.shape[1]
    head_size = width // HEADS
    query_heads = query_box.astype(jnp.float32).reshape(boxes, query_count, HEADS, head_size)
    key_heads = key_box.astype(jnp.float32).reshape(boxes, key_count, HEADS, head_size)
    value_heads = value_box.astype(jnp.float32).reshape(boxes, key_count, HEADS, head_size)
    scores = jnp.einsum("bqhd,bkhd->bhqk", query_heads, key_heads) * (head_size ** -0.5)
    scores = jnp.where(allowed[:, None, None, :], scores, masked_score)
    largest = jnp.max(scores, axis=-1)
    shifted = jnp.exp(scores - largest[..., None])
    totals = weight * jnp.sum(shifted, axis=-1)
    rounded = lax.optimization_barrier(shifted.astype(jnp.bfloat16)).astype(jnp.float32)
    numerators = weight * jnp.einsum("bhqk,bkhd->bqhd", rounded, value_heads)
    return largest, totals, numerators


def level_terms(query_rows, key_rows, value_rows, offsets, weight, parity):
    width = query_rows.shape[1]
    boxes = query_rows.shape[0] // BLOCK
    query_boxes = query_rows.reshape(boxes, BLOCK, width)
    key_boxes = jnp.pad(key_rows.reshape(boxes, BLOCK, width), ((3, 3), (0, 0), (0, 0)))
    value_boxes = jnp.pad(value_rows.reshape(boxes, BLOCK, width), ((3, 3), (0, 0), (0, 0)))
    group = min(boxes, 16)

    def one_group(first_box):
        box_numbers = first_box + jnp.arange(group, dtype=jnp.int32)
        picked = lax.dynamic_slice_in_dim(query_boxes, first_box, group, 0)
        gathered_keys = []
        gathered_values = []
        allowed = []
        for offset in offsets:
            start_row = (first_box + 3 + offset).astype(jnp.int32)
            gathered_keys.append(lax.dynamic_slice_in_dim(key_boxes, start_row, group, 0))
            gathered_values.append(lax.dynamic_slice_in_dim(value_boxes, start_row, group, 0))
            inside = (box_numbers + offset >= 0) & (box_numbers + offset < boxes)
            if parity and offset == 3:
                inside = inside & (box_numbers % 2 == 0)
            if parity and offset == -3:
                inside = inside & (box_numbers % 2 == 1)
            allowed.append(jnp.broadcast_to(inside[:, None], (group, BLOCK)))
        return attend(picked, jnp.concatenate(gathered_keys, axis=1), jnp.concatenate(gathered_values, axis=1), jnp.concatenate(allowed, axis=1), weight)

    group_starts = jnp.arange(boxes // group, dtype=jnp.int32) * group
    largest, totals, numerators = lax.map(one_group, group_starts)
    largest = largest.reshape(boxes, HEADS, BLOCK).transpose(0, 2, 1).reshape(boxes * BLOCK, HEADS)
    totals = totals.reshape(boxes, HEADS, BLOCK).transpose(0, 2, 1).reshape(boxes * BLOCK, HEADS)
    numerators = numerators.reshape(boxes * BLOCK, HEADS, width // HEADS)
    return largest, totals, numerators


def combine_level(running, terms, factor):
    largest, totals, numerators = terms
    if factor > 1:
        largest = jnp.repeat(largest, factor, axis=0)
        totals = jnp.repeat(totals, factor, axis=0)
        numerators = jnp.repeat(numerators, factor, axis=0)
    run_peak, run_total, run_numer = running
    newest = jnp.maximum(run_peak, largest)
    keep_old = jnp.exp(run_peak - newest)
    keep_new = jnp.exp(largest - newest)
    return newest, run_total * keep_old + totals * keep_new, run_numer * keep_old[..., None] + numerators * keep_new[..., None]


def reference(query_vectors, key_vectors, value_vectors):
    length = query_vectors.shape[0]
    levels = (length // BLOCK).bit_length() - 1
    running = level_terms(query_vectors, key_vectors, value_vectors, (-1, 0, 1), 1.0, False)
    coarse_query, coarse_key, coarse_value = query_vectors, key_vectors, value_vectors
    for height in range(1, levels - 1):
        coarse_query = halve(coarse_query)
        coarse_key = halve(coarse_key)
        coarse_value = halve(coarse_value)
        terms = level_terms(coarse_query, coarse_key, coarse_value, (-3, -2, 2, 3), float(2 ** height), True)
        running = combine_level(running, terms, 2 ** height)
    run_peak, run_total, run_numer = running
    return (run_numer / run_total[..., None]).reshape(length, -1).astype(jnp.bfloat16)
```

```python
import functools
import math

import jax
import jax.numpy as jnp
from jax import lax
from jax.experimental import pallas as pl
from jax.experimental.pallas import tpu as pltpu
from jax.sharding import PartitionSpec as P

MESH = pl.DeviceIdType.MESH
HEADS = 8
BOX = 128
ROWS = 8
MASKED = -1e30
TO_LOG2 = math.log2(math.e) / math.sqrt(128.0)


def pool(rows):
    count = rows.shape[0]
    target = lax.broadcasted_iota(jnp.int32, (count // 2, count), 0)
    source = lax.broadcasted_iota(jnp.int32, (count // 2, count), 1)
    pairs = jnp.where(source // 2 == target, 0.5, 0.0).astype(jnp.bfloat16)
    return jnp.dot(pairs, rows, preferred_element_type=jnp.float32).astype(jnp.bfloat16)


def attend(query, keys, values, biases):
    scores = []
    for key, bias in zip(keys, biases):
        score = lax.dot_general(query, key, (((1,), (1,)), ((), ())), preferred_element_type=jnp.float32) * TO_LOG2
        scores.append(score if bias is None else score + bias)
    peak = jnp.max(functools.reduce(jnp.maximum, scores), axis=1, keepdims=True)
    shifted = [jnp.exp2(score - peak) for score in scores]
    total = jnp.sum(functools.reduce(jnp.add, shifted), axis=1, keepdims=True)
    weights = jnp.concatenate([part.astype(jnp.bfloat16) for part in shifted], axis=1)
    numerator = jnp.dot(weights, jnp.concatenate(values, axis=0), preferred_element_type=jnp.float32)
    return jnp.broadcast_to(peak, numerator.shape), jnp.broadcast_to(total, numerator.shape), numerator


def merge(one, other):
    newest = jnp.maximum(one[0], other[0])
    keep_one = jnp.exp2(one[0] - newest)
    keep_other = jnp.exp2(other[0] - newest)
    return newest, one[1] * keep_one + other[1] * keep_other, one[2] * keep_one + other[2] * keep_other


def kernel(zs, q_hbm, k_hbm, v_hbm, out_ref, source, q0, q1, q2, kv0, kv1, kv2, kv3, kv4, terms0, terms1, spread, done, load_sem, send_sem, recv_sem):
    me = lax.axis_index("ctx")
    z = me // ROWS
    rank = lax.rem(me, ROWS)
    odd = lax.rem(z, 2)

    def ring(step):
        return z * ROWS + lax.rem(rank + step, ROWS)

    def column(other):
        return lax.rem(other + zs, zs) * ROWS + rank

    def mate(other):
        return other + 1 - 2 * lax.rem(other, 2)

    opposite = lax.rem(z + zs // 2, zs)
    mirrored = zs - 1 - z
    has_left = z > 0
    has_right = z < zs - 1
    has_a = z >= 2
    has_b = z < zs - 2
    has_c = ((odd == 0) & (z + 3 < zs)) | ((odd == 1) & (z >= 3))
    has_e = (z < 2) | (z >= zs - 2)
    third = z + 3 - 6 * odd

    loads = [
        pltpu.make_async_copy(ref, source.at[n], load_sem.at[n]) for n, ref in enumerate((k_hbm, v_hbm, q_hbm))
    ]
    for load in loads:
        load.start()
    barrier = pltpu.get_barrier_semaphore()
    for step in range(1, ROWS):
        pl.semaphore_signal(barrier, inc=1, device_id={"ctx": ring(step)}, device_id_type=MESH)
    for step in range(1, zs):
        pl.semaphore_signal(barrier, inc=1, device_id={"ctx": column(z + step)}, device_id_type=MESH)

    def blank(ref, present, start, count):
        @pl.when(jnp.logical_not(present))
        def _():
            ref[:, start : start + count, :] = jnp.zeros((2, count, BOX), jnp.bfloat16)

    blank(kv0, has_left, 0, BOX)
    blank(kv0, has_right, 9 * BOX, BOX)
    blank(kv1, has_left, 0, 2 * BOX)
    blank(kv1, has_right, 6 * BOX, 2 * BOX)
    blank(kv2, has_left, 0, BOX)
    blank(kv2, has_right, 5 * BOX, BOX)
    blank(kv3, has_a, 0, BOX)
    blank(kv3, has_b, BOX, BOX)
    blank(kv3, has_c, 2 * BOX, BOX)
    blank(kv4, has_e, BOX, BOX)

    used = [0]

    def remote(src, dst, device):
        number = used[0]
        used[0] += 1
        return pltpu.make_async_remote_copy(
            src_ref=src,
            dst_ref=dst,
            send_sem=send_sem.at[number],
            recv_sem=recv_sem.at[number],
            device_id={"ctx": device},
            device_id_type=MESH,
        )

    def when(present, action):
        if present is None:
            action()
        else:
            pl.when(present)(action)

    sent = []

    def send(src, dst, device, goes=None, comes=None):
        copy = remote(src, dst, device)
        when(goes, copy.start)
        sent.append((copy, goes))
        return copy, comes

    def arrive(message):
        when(message[1], message[0].wait_recv)

    pl.semaphore_wait(barrier, ROWS - 1 + zs - 1)

    def head(number):
        return pl.ds(pl.multiple_of(number * BOX, BOX), BOX)

    loads[0].wait()
    loads[1].wait()
    kv_in = [
        send(
            source.at[pl.ds(0, 2), :, head(lax.rem(rank + step, ROWS))],
            kv0.at[:, head(rank + 1), :],
            ring(step),
        )
        for step in range(1, ROWS)
    ]
    own_kv = pltpu.make_async_copy(source.at[pl.ds(0, 2), :, head(rank)], kv0.at[:, head(rank + 1), :], load_sem.at[3])
    own_kv.start()
    loads[2].wait()
    q_in = [
        send(source.at[2, :, head(lax.rem(rank + step, ROWS))], q0.at[head(rank), :], ring(step))
        for step in range(1, ROWS)
    ]
    own_q = pltpu.make_async_copy(source.at[2, :, head(rank)], q0.at[head(rank), :], load_sem.at[4])
    own_q.start()

    own_kv.wait()
    for message in kv_in:
        arrive(message)

    def box(ref, kind, start):
        return ref[kind, start * BOX : (start + 1) * BOX, :]

    left0 = send(kv0.at[:, pl.ds(8 * BOX, BOX), :], kv0.at[:, pl.ds(0, BOX), :], column(z + 1), has_right, has_left)
    right0 = send(kv0.at[:, pl.ds(BOX, BOX), :], kv0.at[:, pl.ds(9 * BOX, BOX), :], column(z - 1), has_left, has_right)
    for kind in range(2):
        for n in range(4):
            kv1[kind, (2 + n) * BOX : (3 + n) * BOX, :] = pool(kv0[kind, (2 * n + 1) * BOX : (2 * n + 3) * BOX, :])
    for kind in range(2):
        for n in range(2):
            kv2[kind, (2 + n) * BOX : (3 + n) * BOX, :] = pool(kv1[kind, (2 * n + 2) * BOX : (2 * n + 4) * BOX, :])
        kv3[kind, 3 * BOX : 4 * BOX, :] = pool(kv2[kind, 2 * BOX : 4 * BOX, :])
        kv4[kind, 2 * BOX : 2 * BOX + BOX // 2, :] = pool(kv3[kind, 3 * BOX : 4 * BOX, :])

    own4 = kv4.at[:, pl.ds(2 * BOX, BOX // 2), :]
    half = pl.multiple_of(odd * (BOX // 2), BOX // 2)
    d_in = [
        send(own4, kv4.at[:, pl.ds(half, BOX // 2), :], column(opposite)),
        send(own4, kv4.at[:, pl.ds(half, BOX // 2), :], column(mate(opposite))),
    ]
    e_in = [
        send(own4, kv4.at[:, pl.ds(BOX + half, BOX // 2), :], column(mate(mirrored)), has_e, has_e),
        send(own4, kv4.at[:, pl.ds(BOX + half, BOX // 2), :], column(mirrored), has_e, has_e),
    ]
    own3 = kv3.at[:, pl.ds(3 * BOX, BOX), :]
    c_in = send(own3, kv3.at[:, pl.ds(2 * BOX, BOX), :], column(third), has_c, has_c)
    a_in = send(own3, kv3.at[:, pl.ds(0, BOX), :], column(z + 2), has_b, has_a)
    b_in = send(own3, kv3.at[:, pl.ds(BOX, BOX), :], column(z - 2), has_a, has_b)
    left1 = send(kv1.at[:, pl.ds(4 * BOX, 2 * BOX), :], kv1.at[:, pl.ds(0, 2 * BOX), :], column(z + 1), has_right, has_left)
    right1 = send(kv1.at[:, pl.ds(2 * BOX, 2 * BOX), :], kv1.at[:, pl.ds(6 * BOX, 2 * BOX), :], column(z - 1), has_left, has_right)
    left2 = send(kv2.at[:, pl.ds(2 * BOX, BOX), :], kv2.at[:, pl.ds(0, BOX), :], column(z + 1), has_right, has_left)
    right2 = send(kv2.at[:, pl.ds(3 * BOX, BOX), :], kv2.at[:, pl.ds(5 * BOX, BOX), :], column(z - 1), has_left, has_right)

    def bias(present):
        return jnp.where(present, 0.0, MASKED).astype(jnp.float32)

    left_bias, right_bias = bias(has_left), bias(has_right)

    own_q.wait()
    for message in q_in:
        arrive(message)
    for n in range(4):
        q1[n * BOX : (n + 1) * BOX, :] = pool(q0[2 * n * BOX : (2 * n + 2) * BOX, :])
    for n in range(2):
        q2[n * BOX : (n + 1) * BOX, :] = pool(q1[2 * n * BOX : (2 * n + 2) * BOX, :])
    q3 = pool(q2[...])
    q4 = pool(q3)

    def level(query, ref, boxes, biases):
        return attend(query, [box(ref, 0, b) for b in boxes], [box(ref, 1, b) for b in boxes], biases)

    def keep(ref, n, values):
        for kind in range(3):
            ref[kind, n * BOX : (n + 1) * BOX, :] = values[kind]

    def kept(ref, n):
        return tuple(ref[kind, n * BOX : (n + 1) * BOX, :] for kind in range(3))

    def level0(n):
        biases = [left_bias if n == 0 else None, None, right_bias if n == ROWS - 1 else None]
        keep(terms0, n, level(q0[n * BOX : (n + 1) * BOX, :], kv0, (n, n + 1, n + 2), biases))

    for n in range(1, ROWS - 1):
        level0(n)
    arrive(left0)
    arrive(right0)
    level0(0)
    level0(ROWS - 1)

    def raised(values, height):
        return values[0] + float(height), values[1], values[2]

    arrive(left1)
    arrive(right1)
    for n, boxes in enumerate(((0, 4, 5), (1, 5, 0), (2, 6, 7), (3, 7, 2))):
        biases = [left_bias if b < 2 else right_bias if b >= 6 else None for b in boxes]
        keep(terms1, n, raised(level(q1[n * BOX : (n + 1) * BOX, :], kv1, boxes, biases), 1))
    for kind in range(2):
        kv2[kind, BOX : 2 * BOX, :] = pool(kv1[kind, 0 : 2 * BOX, :])
        kv2[kind, 4 * BOX : 5 * BOX, :] = pool(kv1[kind, 6 * BOX : 8 * BOX, :])
    arrive(left2)
    arrive(right2)

    def doubled(values, slot):
        count = values[0].shape[0]
        for kind in range(3):
            spread[slot, kind, pl.ds(0, count, 2), :] = values[kind]
            spread[slot, kind, pl.ds(1, count, 2), :] = values[kind]
        return tuple(spread[slot, kind, 0 : 2 * count, :] for kind in range(3))

    def split(values, n):
        return tuple(part[n * BOX : (n + 1) * BOX, :] for part in values)

    level2 = []
    for n, boxes in enumerate(((0, 4, 5), (1, 5, 0))):
        biases = [left_bias if b < 2 else right_bias for b in boxes]
        level2.append(raised(level(q2[n * BOX : (n + 1) * BOX, :], kv2, boxes, biases), 2))

    for message in (a_in, b_in, c_in):
        arrive(message)
    level3 = raised(level(q3, kv3, (0, 1, 2), [bias(has_a), bias(has_b), bias(has_c)]), 3)
    for message in d_in + e_in:
        arrive(message)
    level4 = raised(level(q4, kv4, (0, 1), [None, bias(has_e)]), 4)

    coarse = merge(level3, doubled(level4, 0))
    coarse = doubled(coarse, 1)
    for n in range(2):
        two = doubled(merge(level2[n], split(coarse, n)), 2 + n)
        for m in range(2):
            one = doubled(merge(kept(terms1, 2 * n + m), split(two, m)), 4 + 2 * n + m)
            for i in range(2):
                b = 4 * n + 2 * m + i
                _, total, numerator = merge(kept(terms0, b), split(one, i))
                done[b * BOX : (b + 1) * BOX, :] = (numerator / total).astype(jnp.bfloat16)

    back = [
        send(done.at[head(lax.rem(rank + step, ROWS)), :], out_ref.at[:, head(rank)], ring(step))
        for step in range(1, ROWS)
    ]
    own_out = pltpu.make_async_copy(done.at[head(rank), :], out_ref.at[:, head(rank)], load_sem.at[5])
    own_out.start()
    own_out.wait()
    for message in back:
        arrive(message)
    for copy, present in sent:
        when(present, copy.wait_send)


MESSAGES = 3 * (ROWS - 1) + 13


def solution(mesh):
    zs = mesh.shape["ctx"] // ROWS

    def step(q, k, v):
        anywhere = pl.BlockSpec(memory_space=pl.ANY)
        return pl.pallas_call(
            functools.partial(kernel, zs),
            out_shape=jax.ShapeDtypeStruct(q.shape, jnp.bfloat16),
            in_specs=[anywhere] * 3,
            out_specs=pl.BlockSpec(memory_space=pltpu.VMEM),
            scratch_shapes=[
                pltpu.VMEM((3, BOX, HEADS * BOX), jnp.bfloat16),
                pltpu.VMEM((8 * BOX, BOX), jnp.bfloat16),
                pltpu.VMEM((4 * BOX, BOX), jnp.bfloat16),
                pltpu.VMEM((2 * BOX, BOX), jnp.bfloat16),
                pltpu.VMEM((2, 10 * BOX, BOX), jnp.bfloat16),
                pltpu.VMEM((2, 8 * BOX, BOX), jnp.bfloat16),
                pltpu.VMEM((2, 6 * BOX, BOX), jnp.bfloat16),
                pltpu.VMEM((2, 4 * BOX, BOX), jnp.bfloat16),
                pltpu.VMEM((2, 5 * BOX // 2, BOX), jnp.bfloat16),
                pltpu.VMEM((3, 8 * BOX, BOX), jnp.float32),
                pltpu.VMEM((3, 4 * BOX, BOX), jnp.float32),
                pltpu.VMEM((8, 3, 2 * BOX, BOX), jnp.float32),
                pltpu.VMEM((8 * BOX, BOX), jnp.bfloat16),
                pltpu.SemaphoreType.DMA((6,)),
                pltpu.SemaphoreType.DMA((MESSAGES,)),
                pltpu.SemaphoreType.DMA((MESSAGES,)),
            ],
            compiler_params=pltpu.CompilerParams(
                collective_id=0, has_side_effects=True, vmem_limit_bytes=60 * 2**20
            ),
            cost_estimate=pl.CostEstimate(flops=400_000_000, bytes_accessed=2**20, transcendentals=800_000),
            name="attention",
        )(q, k, v)

    spec = P(("doc", "ctx"), None)
    return jax.shard_map(step, mesh=mesh, in_specs=(spec,) * 3, out_specs=spec, check_vma=False)
```

```python
import functools
import math

import jax
import jax.numpy as jnp
from jax import lax
from jax.experimental import pallas as pl
from jax.experimental.pallas import tpu as pltpu
from jax.sharding import PartitionSpec as P

MESH = pl.DeviceIdType.MESH
HEADS = 8
BOX = 128
ROWS = 8
MASKED = -1e30
TO_LOG2 = math.log2(math.e) / math.sqrt(128.0)


def pool(rows):
    count = rows.shape[0]
    target = lax.broadcasted_iota(jnp.int32, (count // 2, count), 0)
    source = lax.broadcasted_iota(jnp.int32, (count // 2, count), 1)
    pairs = jnp.where(source // 2 == target, 0.5, 0.0).astype(jnp.bfloat16)
    return jnp.dot(pairs, rows, preferred_element_type=jnp.float32).astype(jnp.bfloat16)


def attend(query, keys, values, biases):
    scores = []
    for key, bias in zip(keys, biases):
        score = lax.dot_general(query, key, (((1,), (1,)), ((), ())), preferred_element_type=jnp.float32) * TO_LOG2
        scores.append(score if bias is None else score + bias)
    peak = jnp.max(functools.reduce(jnp.maximum, scores), axis=1, keepdims=True)
    shifted = [jnp.exp2(score - peak) for score in scores]
    total = jnp.sum(functools.reduce(jnp.add, shifted), axis=1, keepdims=True)
    weights = jnp.concatenate([part.astype(jnp.bfloat16) for part in shifted], axis=1)
    numerator = jnp.dot(weights, jnp.concatenate(values, axis=0), preferred_element_type=jnp.float32)
    return jnp.broadcast_to(peak, numerator.shape), jnp.broadcast_to(total, numerator.shape), numerator


def merge(one, other):
    newest = jnp.maximum(one[0], other[0])
    keep_one = jnp.exp2(one[0] - newest)
    keep_other = jnp.exp2(other[0] - newest)
    return newest, one[1] * keep_one + other[1] * keep_other, one[2] * keep_one + other[2] * keep_other


def kernel(zs, q_hbm, k_hbm, v_hbm, out_ref, source, far, q0, q1, q2, kv0, kv1, kv2, kv3, kv4, terms, ups, done, load_sem, send_sem, recv_sem, round_sem):
    me = lax.axis_index("ctx")
    z = me // ROWS
    rank = lax.rem(me, ROWS)
    y, core = rank // 2, lax.rem(rank, 2)
    odd = lax.rem(z, 2)

    def ring(turn, flip):
        return 2 * lax.rem(y + turn, 4) + lax.rem(core + flip, 2)

    def column(other):
        return lax.rem(other + zs, zs) * ROWS + rank

    def mate(other):
        return other + 1 - 2 * lax.rem(other, 2)

    peers = [(2, 0), (2, 1), (1, 0), (1, 1), (3, 0), (3, 1), (0, 1)]
    opposite = lax.rem(z + zs // 2, zs)
    mirrored = zs - 1 - z
    has_left = z > 0
    has_right = z < zs - 1
    has_a = z >= 2
    has_b = z < zs - 2
    has_c = ((odd == 0) & (z + 3 < zs)) | ((odd == 1) & (z >= 3))
    has_e = (z < 2) | (z >= zs - 2)

    loads = [
        pltpu.make_async_copy(ref, source.at[n], load_sem.at[n]) for n, ref in enumerate((k_hbm, v_hbm, q_hbm))
    ]
    for load in loads:
        load.start()

    def when(present, action):
        if present is None:
            action()
        else:
            pl.when(present)(action)

    def signal(semaphore, device):
        pl.semaphore_signal(semaphore, inc=1, device_id={"ctx": device}, device_id_type=MESH)

    barrier = pltpu.get_barrier_semaphore()
    for turn, flip in peers:
        signal(barrier, z * ROWS + ring(turn, flip))
    when(has_left, lambda: signal(barrier, column(z - 1)))
    when(has_right, lambda: signal(barrier, column(z + 1)))

    def blank(ref, present, start, count):
        @pl.when(jnp.logical_not(present))
        def _():
            ref[:, start : start + count, :] = jnp.zeros((2, count, BOX), jnp.bfloat16)

    blank(kv0, has_left, 0, BOX)
    blank(kv0, has_right, 9 * BOX, BOX)
    blank(kv1, has_left, 0, 2 * BOX)
    blank(kv1, has_right, 6 * BOX, 2 * BOX)
    blank(kv2, has_left, 0, BOX)
    blank(kv2, has_right, 5 * BOX, BOX)
    blank(kv3, has_a, 0, BOX)
    blank(kv3, has_b, BOX, BOX)
    blank(kv3, has_c, 2 * BOX, BOX)
    blank(kv4, has_e, BOX, BOX)

    used = [0]
    sent = []

    def remote(src, dst, device):
        number = used[0]
        used[0] += 1
        return pltpu.make_async_remote_copy(
            src_ref=src,
            dst_ref=dst,
            send_sem=send_sem.at[number],
            recv_sem=recv_sem.at[number],
            device_id={"ctx": device},
            device_id_type=MESH,
        )

    def send(src, dst, device, goes=None, comes=None):
        copy = remote(src, dst, device)
        when(goes, copy.start)
        sent.append((copy, goes))
        return copy, comes

    def arrive(message):
        when(message[1], message[0].wait_recv)

    def head(number):
        return pl.ds(pl.multiple_of(number * BOX, BOX), BOX)

    third = BOX // 8
    for kind in range(2):
        loads[kind].wait()
        far[kind] = pool(pool(pool(source[kind])))
    pl.semaphore_wait(barrier, ROWS - 1 + (z + zs - 1) // zs + (2 * zs - 2 - z) // zs)

    own_third = pl.ds(pl.multiple_of(3 * BOX + rank * third, third), third)
    far_in = [
        send(far.at[:, :, head(ring(turn, flip))], kv3.at[:, own_third, :], z * ROWS + ring(turn, flip))
        for turn, flip in peers
    ]
    kv_in = {
        (turn, flip): send(
            source.at[pl.ds(0, 2), :, head(ring(turn, flip))], kv0.at[:, head(rank + 1), :], z * ROWS + ring(turn, flip)
        )
        for turn, flip in peers
    }
    own_kv = pltpu.make_async_copy(source.at[pl.ds(0, 2), :, head(rank)], kv0.at[:, head(rank + 1), :], load_sem.at[3])
    own_kv.start()
    loads[2].wait()
    q_in = [
        send(source.at[2, :, head(ring(turn, flip))], q0.at[head(rank), :], z * ROWS + ring(turn, flip))
        for turn, flip in peers
    ]
    own_q = pltpu.make_async_copy(source.at[2, :, head(rank)], q0.at[head(rank), :], load_sem.at[4])
    own_q.start()
    kv3[:, own_third, :] = far[:, :, head(rank)]

    for turn in range(3):
        reach = 1 << turn
        below, above = z >= reach, z < zs - reach
        when(below, lambda: signal(round_sem.at[turn], column(z - reach)))
        when(above, lambda: signal(round_sem.at[turn], column(z + reach)))
        pl.semaphore_wait(round_sem.at[turn], (z + zs - reach) // zs + (2 * zs - 1 - z - reach) // zs)

    for message in far_in:
        arrive(message)
    for kind in range(2):
        kv4[kind, 2 * BOX : 2 * BOX + BOX // 2, :] = pool(kv3[kind, 3 * BOX : 4 * BOX, :])
    own4 = kv4.at[:, pl.ds(2 * BOX, BOX // 2), :]
    half = pl.multiple_of(odd * (BOX // 2), BOX // 2)
    far4_in = [
        send(own4, kv4.at[:, pl.ds(BOX + half, BOX // 2), :], column(mate(mirrored)), has_e, has_e),
        send(own4, kv4.at[:, pl.ds(BOX + half, BOX // 2), :], column(mirrored), has_e, has_e),
        send(own4, kv4.at[:, pl.ds(half, BOX // 2), :], column(opposite)),
        send(own4, kv4.at[:, pl.ds(half, BOX // 2), :], column(mate(opposite))),
    ]
    own3 = kv3.at[:, pl.ds(3 * BOX, BOX), :]
    a_in = send(own3, kv3.at[:, pl.ds(0, BOX), :], column(z + 2), has_b, has_a)
    b_in = send(own3, kv3.at[:, pl.ds(BOX, BOX), :], column(z - 2), has_a, has_b)

    left0 = remote(kv0.at[:, pl.ds(8 * BOX, BOX), :], kv0.at[:, pl.ds(0, BOX), :], column(z + 1))
    right0 = remote(kv0.at[:, pl.ds(BOX, BOX), :], kv0.at[:, pl.ds(9 * BOX, BOX), :], column(z - 1))
    own_kv.wait()
    near1 = []
    for turn in (0, 1, 3, 2):
        chip = lax.rem(y + turn, 4)
        back = (4 - turn) % 4
        for flip in range(2):
            if (back, flip) in kv_in:
                arrive(kv_in[back, flip])
        when((chip == 3) & has_right, left0.start)
        when((chip == 0) & has_left, right0.start)
        pair = pl.ds(pl.multiple_of((2 * chip + 1) * BOX, BOX), 2 * BOX)
        for kind in range(2):
            kv1[kind, head(2 + chip), :] = pool(kv0[kind, pair, :])
        up = chip >= 2
        near1.append(
            send(
                kv1.at[:, head(2 + chip), :],
                kv1.at[:, head(lax.rem(chip + 6, 8)), :],
                column(z - 1 + 2 * (chip // 2)),
                (up & has_right) | (jnp.logical_not(up) & has_left),
                (up & has_left) | (jnp.logical_not(up) & has_right),
            )
        )
    for kind in range(2):
        for n in range(2):
            kv2[kind, (2 + n) * BOX : (3 + n) * BOX, :] = pool(kv1[kind, (2 * n + 2) * BOX : (2 * n + 4) * BOX, :])
    left2 = send(kv2.at[:, pl.ds(2 * BOX, BOX), :], kv2.at[:, pl.ds(0, BOX), :], column(z + 1), has_right, has_left)
    right2 = send(kv2.at[:, pl.ds(3 * BOX, BOX), :], kv2.at[:, pl.ds(5 * BOX, BOX), :], column(z - 1), has_left, has_right)

    arrive(a_in)
    arrive(b_in)
    c_in = send(
        kv3.at[:, head(odd), :],
        kv3.at[:, pl.ds(2 * BOX, BOX), :],
        column(mate(z)),
        ((odd == 0) & has_a) | ((odd == 1) & has_b),
        has_c,
    )

    def bias(present):
        return jnp.where(present, 0.0, MASKED).astype(jnp.float32)

    left_bias, right_bias = bias(has_left), bias(has_right)

    own_q.wait()
    for message in q_in:
        arrive(message)
    for n in range(4):
        q1[n * BOX : (n + 1) * BOX, :] = pool(q0[2 * n * BOX : (2 * n + 2) * BOX, :])
    for n in range(2):
        q2[n * BOX : (n + 1) * BOX, :] = pool(q1[2 * n * BOX : (2 * n + 2) * BOX, :])
    q3 = pool(q2[...])
    q4 = pool(q3)

    def box(ref, kind, start):
        return ref[kind, start * BOX : (start + 1) * BOX, :]

    def level(query, ref, boxes, biases):
        return attend(query, [box(ref, 0, b) for b in boxes], [box(ref, 1, b) for b in boxes], biases)

    def keep(n, values):
        for kind in range(3):
            terms[kind, n * BOX : (n + 1) * BOX, :] = values[kind]

    def kept(n):
        return tuple(terms[kind, n * BOX : (n + 1) * BOX, :] for kind in range(3))

    def level0(n):
        biases = [left_bias if n == 0 else None, None, right_bias if n == ROWS - 1 else None]
        keep(n, level(q0[n * BOX : (n + 1) * BOX, :], kv0, (n, n + 1, n + 2), biases))

    def raised(values, height):
        return values[0] + float(height), values[1], values[2]

    def repeated(values, start, times):
        count = values[0].shape[0]
        for kind in range(3):
            for turn in range(times):
                ups[kind, pl.ds(start + turn, count, times), :] = values[kind]

    def risen(start, count):
        return tuple(ups[kind, start : start + count, :] for kind in range(3))

    for n in range(1, ROWS - 1):
        level0(n)
    for message in near1:
        arrive(message)
    for kind in range(2):
        kv2[kind, BOX : 2 * BOX, :] = pool(kv1[kind, 0 : 2 * BOX, :])
        kv2[kind, 4 * BOX : 5 * BOX, :] = pool(kv1[kind, 6 * BOX : 8 * BOX, :])
    level1 = []
    for n, boxes in enumerate(((0, 4, 5), (1, 5, 0), (2, 6, 7), (3, 7, 2))):
        biases = [left_bias if b < 2 else right_bias if b >= 6 else None for b in boxes]
        level1.append(raised(level(q1[n * BOX : (n + 1) * BOX, :], kv1, boxes, biases), 1))
    when(has_left, left0.wait_recv)
    when(has_right, right0.wait_recv)
    level0(0)
    level0(ROWS - 1)
    arrive(left2)
    arrive(right2)
    for n, boxes in enumerate(((0, 4, 5), (1, 5, 0))):
        biases = [left_bias if b < 2 else right_bias for b in boxes]
        level2 = raised(level(q2[n * BOX : (n + 1) * BOX, :], kv2, boxes, biases), 2)
        repeated(level2, 2 * n * BOX, 2)
        for m in range(2):
            repeated(merge(level1[2 * n + m], risen((2 * n + m) * BOX, BOX)), 8 * BOX + 2 * (2 * n + m) * BOX, 2)
    for n in range(ROWS):
        keep(n, merge(kept(n), risen((8 + n) * BOX, BOX)))

    arrive(c_in)
    level3 = raised(level(q3, kv3, (0, 1, 2), [bias(has_a), bias(has_b), bias(has_c)]), 3)
    for message in far4_in:
        arrive(message)
    repeated(raised(level(q4, kv4, (0, 1), [None, bias(has_e)]), 4), 0, 2)
    repeated(merge(level3, risen(0, BOX)), 8 * BOX, 8)

    def finish(number):
        fine = tuple(terms[kind, head(number), :] for kind in range(3))
        coarse = tuple(ups[kind, head(8 + number), :] for kind in range(3))
        _, total, numerator = merge(fine, coarse)
        done[head(number), :] = (numerator / total).astype(jnp.bfloat16)

    home = []
    for turn, flip in peers:
        number = ring(turn, flip)
        finish(number)
        home.append(send(done.at[head(number), :], out_ref.at[:, head(rank)], z * ROWS + number))
    finish(rank)
    own_out = pltpu.make_async_copy(done.at[head(rank), :], out_ref.at[:, head(rank)], load_sem.at[5])
    own_out.start()
    own_out.wait()
    for message in home:
        arrive(message)
    for copy, goes in sent:
        when(goes, copy.wait_send)
    when(has_right, left0.wait_send)
    when(has_left, right0.wait_send)


MESSAGES = 4 * (ROWS - 1) + 15


def solution(mesh):
    zs = mesh.shape["ctx"] // ROWS

    def step(q, k, v):
        anywhere = pl.BlockSpec(memory_space=pl.ANY)
        return pl.pallas_call(
            functools.partial(kernel, zs),
            out_shape=jax.ShapeDtypeStruct(q.shape, jnp.bfloat16),
            in_specs=[anywhere] * 3,
            out_specs=pl.BlockSpec(memory_space=pltpu.VMEM),
            scratch_shapes=[
                pltpu.VMEM((3, BOX, HEADS * BOX), jnp.bfloat16),
                pltpu.VMEM((2, BOX // 8, HEADS * BOX), jnp.bfloat16),
                pltpu.VMEM((8 * BOX, BOX), jnp.bfloat16),
                pltpu.VMEM((4 * BOX, BOX), jnp.bfloat16),
                pltpu.VMEM((2 * BOX, BOX), jnp.bfloat16),
                pltpu.VMEM((2, 10 * BOX, BOX), jnp.bfloat16),
                pltpu.VMEM((2, 8 * BOX, BOX), jnp.bfloat16),
                pltpu.VMEM((2, 6 * BOX, BOX), jnp.bfloat16),
                pltpu.VMEM((2, 4 * BOX, BOX), jnp.bfloat16),
                pltpu.VMEM((2, 5 * BOX // 2, BOX), jnp.bfloat16),
                pltpu.VMEM((3, 8 * BOX, BOX), jnp.float32),
                pltpu.VMEM((3, 16 * BOX, BOX), jnp.float32),
                pltpu.VMEM((8 * BOX, BOX), jnp.bfloat16),
                pltpu.SemaphoreType.DMA((6,)),
                pltpu.SemaphoreType.DMA((MESSAGES,)),
                pltpu.SemaphoreType.DMA((MESSAGES,)),
                pltpu.SemaphoreType.REGULAR((3,)),
            ],
            compiler_params=pltpu.CompilerParams(
                collective_id=0, has_side_effects=True, vmem_limit_bytes=60 * 2**20
            ),
            cost_estimate=pl.CostEstimate(flops=400_000_000, bytes_accessed=2**20, transcendentals=800_000),
            name="attention",
        )(q, k, v)

    spec = P(("doc", "ctx"), None)
    return jax.shard_map(step, mesh=mesh, in_specs=(spec,) * 3, out_specs=spec, check_vma=False)
```

```python
import functools
import math

import jax
import jax.numpy as jnp
from jax import lax
from jax.experimental import pallas as pl
from jax.experimental.pallas import tpu as pltpu
from jax.sharding import PartitionSpec as P

MESH = pl.DeviceIdType.MESH
HEADS = 8
BOX = 128
ROWS = 8
MASKED = -1e30
TO_LOG2 = math.log2(math.e) / math.sqrt(128.0)


def pool(rows):
    count = rows.shape[0]
    target = lax.broadcasted_iota(jnp.int32, (count // 2, count), 0)
    source = lax.broadcasted_iota(jnp.int32, (count // 2, count), 1)
    pairs = jnp.where(source // 2 == target, 0.5, 0.0).astype(jnp.bfloat16)
    return jnp.dot(pairs, rows, preferred_element_type=jnp.float32).astype(jnp.bfloat16)


def attend(query, keys, values, biases):
    scores = []
    for key, bias in zip(keys, biases):
        score = lax.dot_general(query, key, (((1,), (1,)), ((), ())), preferred_element_type=jnp.float32) * TO_LOG2
        scores.append(score if bias is None else score + bias)
    peak = jnp.max(functools.reduce(jnp.maximum, scores), axis=1, keepdims=True)
    shifted = [jnp.exp2(score - peak) for score in scores]
    total = jnp.sum(functools.reduce(jnp.add, shifted), axis=1, keepdims=True)
    weights = jnp.concatenate([part.astype(jnp.bfloat16) for part in shifted], axis=1)
    numerator = jnp.dot(weights, jnp.concatenate(values, axis=0), preferred_element_type=jnp.float32)
    return jnp.broadcast_to(peak, numerator.shape), jnp.broadcast_to(total, numerator.shape), numerator


def merge(one, other):
    newest = jnp.maximum(one[0], other[0])
    keep_one = jnp.exp2(one[0] - newest)
    keep_other = jnp.exp2(other[0] - newest)
    return newest, one[1] * keep_one + other[1] * keep_other, one[2] * keep_one + other[2] * keep_other


def kernel(zs, q_hbm, k_hbm, v_hbm, out_hbm, source, half1, far, near, relay, q1, q2, kv1, kv2, kv3, kv4, terms, ups, parcel, inbox, done, load_sem, send_sem, recv_sem, round_sem):
    me = lax.axis_index("ctx")
    z = me // ROWS
    rank = lax.rem(me, ROWS)
    y, core = rank // 2, lax.rem(rank, 2)
    odd = lax.rem(z, 2)

    def ring(turn, flip):
        return 2 * lax.rem(y + turn, 4) + lax.rem(core + flip, 2)

    def column(other):
        return lax.rem(other + zs, zs) * ROWS + rank

    def mate(other):
        return other + 1 - 2 * lax.rem(other, 2)

    peers = [(2, 0), (2, 1), (1, 0), (1, 1), (3, 0), (3, 1), (0, 1)]
    opposite = lax.rem(z + zs // 2, zs)
    mirrored = zs - 1 - z
    has_left = z > 0
    has_right = z < zs - 1
    has_a = z >= 2
    has_b = z < zs - 2
    has_c = ((odd == 0) & (z + 3 < zs)) | ((odd == 1) & (z >= 3))
    has_e = (z < 2) | (z >= zs - 2)

    loads = [
        pltpu.make_async_copy(ref, source.at[n], load_sem.at[n]) for n, ref in enumerate((k_hbm, v_hbm, q_hbm))
    ]
    for load in loads:
        load.start()

    def when(present, action):
        if present is None:
            action()
        else:
            pl.when(present)(action)

    def signal(semaphore, device):
        pl.semaphore_signal(semaphore, inc=1, device_id={"ctx": device}, device_id_type=MESH)

    barrier = pltpu.get_barrier_semaphore()
    for turn, flip in peers:
        signal(barrier, z * ROWS + ring(turn, flip))
    when(has_left, lambda: signal(barrier, column(z - 1)))
    when(has_right, lambda: signal(barrier, column(z + 1)))

    def blank(ref, present, start, count):
        @pl.when(jnp.logical_not(present))
        def _():
            ref[:, start : start + count, :] = jnp.zeros((2, count, BOX), jnp.bfloat16)

    blank(kv1, has_left, 0, 2 * BOX)
    blank(kv1, has_right, 6 * BOX, 2 * BOX)
    blank(kv2, has_left, 0, BOX)
    blank(kv2, has_right, 5 * BOX, BOX)
    blank(kv3, has_a, 0, BOX)
    blank(kv3, has_b, BOX, BOX)
    blank(kv3, has_c, 2 * BOX, BOX)
    blank(kv4, has_e, BOX, BOX)

    starts = (z == 0) & (rank == 0)
    ends = (z == zs - 1) & (rank == ROWS - 1)

    @pl.when(starts)
    def _():
        near[0] = jnp.zeros(near.shape[1:], jnp.bfloat16)

    @pl.when(ends)
    def _():
        near[1] = jnp.zeros(near.shape[1:], jnp.bfloat16)

    used = [0]
    sent = []

    def remote(src, dst, device):
        number = used[0]
        used[0] += 1
        return pltpu.make_async_remote_copy(
            src_ref=src,
            dst_ref=dst,
            send_sem=send_sem.at[number],
            recv_sem=recv_sem.at[number],
            device_id={"ctx": device},
            device_id_type=MESH,
        )

    def send(src, dst, device, goes=None, comes=None):
        copy = remote(src, dst, device)
        when(goes, copy.start)
        sent.append((copy, goes))
        return copy, comes

    def arrive(message):
        when(message[1], message[0].wait_recv)

    def head(number):
        return pl.ds(pl.multiple_of(number * BOX, BOX), BOX)

    third = BOX // 8
    for kind in range(2):
        loads[kind].wait()
        half1[kind] = pool(source[kind])
        far[kind] = pool(pool(half1[kind]))
    pl.semaphore_wait(barrier, ROWS - 1 + (z + zs - 1) // zs + (2 * zs - 2 - z) // zs)

    own_third = pl.ds(pl.multiple_of(3 * BOX + rank * third, third), third)
    own_half = pl.ds(pl.multiple_of(2 * BOX + rank * (BOX // 2), BOX // 2), BOX // 2)
    own_query = pl.ds(pl.multiple_of(rank * (BOX // 2), BOX // 2), BOX // 2)
    far_in = [
        send(far.at[:, :, head(ring(turn, flip))], kv3.at[:, own_third, :], z * ROWS + ring(turn, flip))
        for turn, flip in peers
    ]
    kv_in = {
        (turn, flip): send(
            half1.at[pl.ds(0, 2), :, head(ring(turn, flip))], kv1.at[:, own_half, :], z * ROWS + ring(turn, flip)
        )
        for turn, flip in peers
    }
    loads[2].wait()
    half1[2] = pool(source[2])
    q_in = [
        send(half1.at[2, :, head(ring(turn, flip))], q1.at[own_query, :], z * ROWS + ring(turn, flip))
        for turn, flip in peers
    ]
    last = rank // (ROWS - 1)
    at_end = (rank == 0) | (rank == ROWS - 1)
    towards = (last == 1) & has_right | (rank == 0) & has_left
    behind = (last == 1) & has_left | (rank == 0) & has_right
    relay_in = send(source.at[pl.ds(0, 2)], relay, column(z - 1 + 2 * last), towards, behind)

    kv3[:, own_third, :] = far[:, :, head(rank)]
    kv1[:, own_half, :] = half1[0:2, :, head(rank)]
    q1[own_query, :] = half1[2, :, head(rank)]

    def tell(turn):
        reach = 1 << turn
        when(z >= reach, lambda: signal(round_sem.at[turn], column(z - reach)))
        when(z < zs - reach, lambda: signal(round_sem.at[turn], column(z + reach)))

    def hear(turn):
        reach = 1 << turn
        pl.semaphore_wait(round_sem.at[turn], (z + zs - reach) // zs + (2 * zs - 1 - z - reach) // zs)

    tell(0)
    hear(0)
    tell(1)
    for message in far_in:
        arrive(message)
    own3 = kv3.at[:, pl.ds(3 * BOX, BOX), :]
    a_in = send(own3, kv3.at[:, pl.ds(0, BOX), :], column(z + 2), has_b, has_a)
    b_in = send(own3, kv3.at[:, pl.ds(BOX, BOX), :], column(z - 2), has_a, has_b)
    for kind in range(2):
        kv4[kind, 2 * BOX : 2 * BOX + BOX // 2, :] = pool(kv3[kind, 3 * BOX : 4 * BOX, :])
    hear(1)
    tell(2)
    own4 = kv4.at[:, pl.ds(2 * BOX, BOX // 2), :]
    half = pl.multiple_of(odd * (BOX // 2), BOX // 2)
    far4 = [
        (remote(own4, kv4.at[:, pl.ds(BOX + half, BOX // 2), :], column(mate(mirrored))), has_e),
        (remote(own4, kv4.at[:, pl.ds(BOX + half, BOX // 2), :], column(mirrored)), has_e),
        (remote(own4, kv4.at[:, pl.ds(half, BOX // 2), :], column(opposite)), z >= 0),
        (remote(own4, kv4.at[:, pl.ds(half, BOX // 2), :], column(mate(opposite))), z >= 0),
    ]
    sent.extend(far4)

    def send_far4(chosen):
        when(chosen, lambda: hear(2))
        for copy, goes in far4:
            when(chosen & goes, copy.start)

    send_far4(z >= zs // 2)
    near1 = []
    for turn in (0, 1, 3, 2):
        chip = lax.rem(y + turn, 4)
        back = (4 - turn) % 4
        for flip in range(2):
            if (back, flip) in kv_in:
                arrive(kv_in[back, flip])
        up = chip >= 2
        near1.append(
            send(
                kv1.at[:, head(2 + chip), :],
                kv1.at[:, head(lax.rem(chip + 6, 8)), :],
                column(z - 1 + 2 * (chip // 2)),
                (up & has_right) | (jnp.logical_not(up) & has_left),
                (up & has_left) | (jnp.logical_not(up) & has_right),
            )
        )
    for kind in range(2):
        for n in range(2):
            kv2[kind, (2 + n) * BOX : (3 + n) * BOX, :] = pool(kv1[kind, (2 * n + 2) * BOX : (2 * n + 4) * BOX, :])
    left2 = send(kv2.at[:, pl.ds(2 * BOX, BOX), :], kv2.at[:, pl.ds(0, BOX), :], column(z + 1), has_right, has_left)
    right2 = send(kv2.at[:, pl.ds(3 * BOX, BOX), :], kv2.at[:, pl.ds(5 * BOX, BOX), :], column(z - 1), has_left, has_right)

    send_far4(z < zs // 2)

    right0 = send(source.at[pl.ds(0, 2)], near.at[0], me + 1, rank < ROWS - 1, rank > 0)
    left0 = send(source.at[pl.ds(0, 2)], near.at[1], me - 1, rank > 0, rank < ROWS - 1)
    arrive(relay_in)
    around0 = send(relay, near.at[1 - last], z * ROWS + ROWS - 1 - rank, behind, towards)

    arrive(a_in)
    arrive(b_in)
    c_in = send(
        kv3.at[:, head(odd), :],
        kv3.at[:, pl.ds(2 * BOX, BOX), :],
        column(mate(z)),
        ((odd == 0) & has_a) | ((odd == 1) & has_b),
        has_c,
    )

    def bias(present):
        return jnp.where(present, 0.0, MASKED).astype(jnp.float32)

    left_bias, right_bias = bias(has_left), bias(has_right)

    for message in q_in:
        arrive(message)
    for n in range(2):
        q2[n * BOX : (n + 1) * BOX, :] = pool(q1[2 * n * BOX : (2 * n + 2) * BOX, :])
    q3 = pool(q2[...])
    q4 = pool(q3)

    def box(ref, kind, start):
        return ref[kind, start * BOX : (start + 1) * BOX, :]

    def level(query, ref, boxes, biases):
        return attend(query, [box(ref, 0, b) for b in boxes], [box(ref, 1, b) for b in boxes], biases)

    def raised(values, height):
        return values[0] + float(height), values[1], values[2]

    def repeated(values, start, times):
        count = values[0].shape[0]
        for kind in range(3):
            for turn in range(times):
                ups[kind, pl.ds(start + turn, count, times), :] = values[kind]

    def risen(start, count):
        return tuple(ups[kind, start : start + count, :] for kind in range(3))

    for message in near1:
        arrive(message)
    for kind in range(2):
        kv2[kind, BOX : 2 * BOX, :] = pool(kv1[kind, 0 : 2 * BOX, :])
        kv2[kind, 4 * BOX : 5 * BOX, :] = pool(kv1[kind, 6 * BOX : 8 * BOX, :])
    level1 = []
    for n, boxes in enumerate(((0, 4, 5), (1, 5, 0), (2, 6, 7), (3, 7, 2))):
        biases = [left_bias if b < 2 else right_bias if b >= 6 else None for b in boxes]
        level1.append(raised(level(q1[n * BOX : (n + 1) * BOX, :], kv1, boxes, biases), 1))
    arrive(left2)
    arrive(right2)
    for n, boxes in enumerate(((0, 4, 5), (1, 5, 0))):
        biases = [left_bias if b < 2 else right_bias for b in boxes]
        level2 = raised(level(q2[n * BOX : (n + 1) * BOX, :], kv2, boxes, biases), 2)
        repeated(level2, 2 * n * BOX, 2)
        for m in range(2):
            merged = merge(level1[2 * n + m], risen((2 * n + m) * BOX, BOX))
            for kind in range(3):
                terms[kind, (2 * n + m) * BOX : (2 * n + m + 1) * BOX, :] = merged[kind]

    arrive(c_in)
    level3 = raised(level(q3, kv3, (0, 1, 2), [bias(has_a), bias(has_b), bias(has_c)]), 3)
    for message in far4:
        arrive(message)
    repeated(raised(level(q4, kv4, (0, 1), [None, bias(has_e)]), 4), 0, 2)
    repeated(merge(level3, risen(0, BOX)), 4 * BOX, 4)

    here = lax.broadcasted_iota(jnp.int32, (BOX // 2, BOX), 0) == lax.broadcasted_iota(jnp.int32, (BOX // 2, BOX), 1)
    line = lax.broadcasted_iota(jnp.int32, (8, BOX), 0)

    def finish(number, box_out):
        rows = pl.ds(pl.multiple_of(number * (BOX // 2), BOX // 2), BOX // 2)
        rows_up = pl.ds(pl.multiple_of(4 * BOX + number * (BOX // 2), BOX // 2), BOX // 2)
        peak, total, numerator = merge(
            tuple(terms[kind, rows, :] for kind in range(3)), tuple(ups[kind, rows_up, :] for kind in range(3))
        )
        peak_row, total_row = (
            jnp.sum(jnp.where(here, part, 0.0), axis=0, keepdims=True) for part in (peak, total)
        )
        box_out[0 : BOX // 2, :] = numerator
        box_out[BOX // 2 :, :] = jnp.where(line == 0, peak_row, jnp.where(line == 1, total_row, 0.0))

    home = {}
    for n, (turn, flip) in enumerate(peers):
        finish(ring(turn, flip), parcel.at[n])
        home[turn, flip] = send(parcel.at[n], inbox.at[rank], z * ROWS + ring(turn, flip))
    finish(rank, inbox.at[rank])

    arrive(right0)
    arrive(left0)
    arrive(around0)
    start_bias, end_bias = bias(jnp.logical_not(starts)), bias(jnp.logical_not(ends))
    for n in range(HEADS):
        columns = slice(n * BOX, (n + 1) * BOX)
        values = attend(
            source[2, :, columns],
            [near[0, 0, :, columns], source[0, :, columns], near[1, 0, :, columns]],
            [near[0, 1, :, columns], source[1, :, columns], near[1, 1, :, columns]],
            [start_bias, None, end_bias],
        )
        for kind in range(3):
            terms[kind, n * BOX : (n + 1) * BOX, :] = values[kind]

    out_copies = []
    for n, (turn, flip) in enumerate([(0, 0)] + peers[::-1]):
        if n:
            arrive(home[turn, flip])
        number = ring((4 - turn) % 4, flip)
        got = inbox.at[number]
        rows = got[BOX // 2 :, :]
        coarse = [
            jnp.broadcast_to(
                jnp.sum(jnp.where(here, rows[row : row + 1, :], 0.0), axis=1, keepdims=True), (BOX // 2, BOX)
            )
            for row in range(2)
        ]
        repeated((coarse[0], coarse[1], got[0 : BOX // 2, :]), n * BOX, 2)
        fine = tuple(terms[kind, head(number), :] for kind in range(3))
        _, total, numerator = merge(fine, risen(n * BOX, BOX))
        done[:, head(number)] = (numerator / total).astype(jnp.bfloat16)
        copy = pltpu.make_async_copy(done.at[:, head(number)], out_hbm.at[:, head(number)], load_sem.at[3 + n])
        copy.start()
        out_copies.append(copy)
    for copy, goes in sent:
        when(goes, copy.wait_send)
    for copy in out_copies:
        copy.wait()


MESSAGES = 4 * (ROWS - 1) + 17


def solution(mesh):
    zs = mesh.shape["ctx"] // ROWS

    def step(q, k, v):
        anywhere = pl.BlockSpec(memory_space=pl.ANY)
        return pl.pallas_call(
            functools.partial(kernel, zs),
            out_shape=jax.ShapeDtypeStruct(q.shape, jnp.bfloat16),
            in_specs=[anywhere] * 3,
            out_specs=anywhere,
            scratch_shapes=[
                pltpu.VMEM((3, BOX, HEADS * BOX), jnp.bfloat16),
                pltpu.VMEM((3, BOX // 2, HEADS * BOX), jnp.bfloat16),
                pltpu.VMEM((2, BOX // 8, HEADS * BOX), jnp.bfloat16),
                pltpu.VMEM((2, 2, BOX, HEADS * BOX), jnp.bfloat16),
                pltpu.VMEM((2, BOX, HEADS * BOX), jnp.bfloat16),
                pltpu.VMEM((4 * BOX, BOX), jnp.bfloat16),
                pltpu.VMEM((2 * BOX, BOX), jnp.bfloat16),
                pltpu.VMEM((2, 8 * BOX, BOX), jnp.bfloat16),
                pltpu.VMEM((2, 6 * BOX, BOX), jnp.bfloat16),
                pltpu.VMEM((2, 4 * BOX, BOX), jnp.bfloat16),
                pltpu.VMEM((2, 5 * BOX // 2, BOX), jnp.bfloat16),
                pltpu.VMEM((3, 8 * BOX, BOX), jnp.float32),
                pltpu.VMEM((3, 8 * BOX, BOX), jnp.float32),
                pltpu.VMEM((ROWS - 1, BOX // 2 + 8, BOX), jnp.float32),
                pltpu.VMEM((ROWS, BOX // 2 + 8, BOX), jnp.float32),
                pltpu.VMEM((BOX, HEADS * BOX), jnp.bfloat16),
                pltpu.SemaphoreType.DMA((3 + HEADS,)),
                pltpu.SemaphoreType.DMA((MESSAGES,)),
                pltpu.SemaphoreType.DMA((MESSAGES,)),
                pltpu.SemaphoreType.REGULAR((3,)),
            ],
            compiler_params=pltpu.CompilerParams(
                collective_id=0, has_side_effects=True, vmem_limit_bytes=60 * 2**20
            ),
            cost_estimate=pl.CostEstimate(flops=400_000_000, bytes_accessed=2**20, transcendentals=800_000),
            name="attention",
        )(q, k, v)

    spec = P(("doc", "ctx"), None)
    return jax.shard_map(step, mesh=mesh, in_specs=(spec,) * 3, out_specs=spec, check_vma=False)
```

```python
import functools
import math

import jax
import jax.numpy as jnp
from jax import lax
from jax.experimental import pallas as pl
from jax.experimental.pallas import tpu as pltpu
from jax.sharding import PartitionSpec as P

MESH = pl.DeviceIdType.MESH
HEADS = 8
BOX = 128
ROWS = 8
MASKED = -1e30
TO_LOG2 = math.log2(math.e) / math.sqrt(128.0)


def pool(rows):
    count = rows.shape[0]
    target = lax.broadcasted_iota(jnp.int32, (count // 2, count), 0)
    source = lax.broadcasted_iota(jnp.int32, (count // 2, count), 1)
    pairs = jnp.where(source // 2 == target, 0.5, 0.0).astype(jnp.bfloat16)
    return jnp.dot(pairs, rows, preferred_element_type=jnp.float32).astype(jnp.bfloat16)


def attend(query, keys, values, biases):
    scores = []
    for key, bias in zip(keys, biases):
        score = lax.dot_general(query, key, (((1,), (1,)), ((), ())), preferred_element_type=jnp.float32) * TO_LOG2
        scores.append(score if bias is None else score + bias)
    peak = jnp.max(functools.reduce(jnp.maximum, scores), axis=1, keepdims=True)
    shifted = [jnp.exp2(score - peak) for score in scores]
    total = jnp.sum(functools.reduce(jnp.add, shifted), axis=1, keepdims=True)
    weights = jnp.concatenate([part.astype(jnp.bfloat16) for part in shifted], axis=1)
    numerator = jnp.dot(weights, jnp.concatenate(values, axis=0), preferred_element_type=jnp.float32)
    return jnp.broadcast_to(peak, numerator.shape), jnp.broadcast_to(total, numerator.shape), numerator


def merge(one, other):
    newest = jnp.maximum(one[0], other[0])
    keep_one = jnp.exp2(one[0] - newest)
    keep_other = jnp.exp2(other[0] - newest)
    return newest, one[1] * keep_one + other[1] * keep_other, one[2] * keep_one + other[2] * keep_other


def kernel(zs, q_hbm, k_hbm, v_hbm, out_ref, source, half1, far, near, relay, q1, q2, kv1, kv2, kv3, kv4, terms, ups, parcel, inbox, load_sem, send_sem, recv_sem, round_sem):
    me = lax.axis_index("ctx")
    z = me // ROWS
    rank = lax.rem(me, ROWS)
    y, core = rank // 2, lax.rem(rank, 2)
    odd = lax.rem(z, 2)

    def ring(turn, flip):
        return 2 * lax.rem(y + turn, 4) + lax.rem(core + flip, 2)

    def column(other):
        return lax.rem(other + zs, zs) * ROWS + rank

    def mate(other):
        return other + 1 - 2 * lax.rem(other, 2)

    peers = [(2, 0), (2, 1), (1, 0), (1, 1), (3, 0), (3, 1), (0, 1)]
    opposite = lax.rem(z + zs // 2, zs)
    mirrored = zs - 1 - z
    has_left = z > 0
    has_right = z < zs - 1
    has_a = z >= 2
    has_b = z < zs - 2
    has_c = ((odd == 0) & (z + 3 < zs)) | ((odd == 1) & (z >= 3))
    has_e = (z < 2) | (z >= zs - 2)

    loads = [
        pltpu.make_async_copy(ref, source.at[n], load_sem.at[n]) for n, ref in enumerate((k_hbm, v_hbm, q_hbm))
    ]
    for load in loads:
        load.start()

    def when(present, action):
        if present is None:
            action()
        else:
            pl.when(present)(action)

    def signal(semaphore, device):
        pl.semaphore_signal(semaphore, inc=1, device_id={"ctx": device}, device_id_type=MESH)

    barrier = pltpu.get_barrier_semaphore()
    for turn, flip in peers:
        signal(barrier, z * ROWS + ring(turn, flip))
    when(has_left, lambda: signal(barrier, column(z - 1)))
    when(has_right, lambda: signal(barrier, column(z + 1)))

    def blank(ref, present, start, count):
        @pl.when(jnp.logical_not(present))
        def _():
            ref[:, start : start + count, :] = jnp.zeros((2, count, BOX), jnp.bfloat16)

    blank(kv1, has_left, 0, 2 * BOX)
    blank(kv1, has_right, 6 * BOX, 2 * BOX)
    blank(kv2, has_left, 0, BOX)
    blank(kv2, has_right, 5 * BOX, BOX)
    blank(kv3, has_a, 0, BOX)
    blank(kv3, has_b, BOX, BOX)
    blank(kv3, has_c, 2 * BOX, BOX)
    blank(kv4, has_e, BOX, BOX)

    starts = (z == 0) & (rank == 0)
    ends = (z == zs - 1) & (rank == ROWS - 1)

    @pl.when(starts)
    def _():
        near[0] = jnp.zeros(near.shape[1:], jnp.bfloat16)

    @pl.when(ends)
    def _():
        near[1] = jnp.zeros(near.shape[1:], jnp.bfloat16)

    used = [0]
    sent = []

    def remote(src, dst, device):
        number = used[0]
        used[0] += 1
        return pltpu.make_async_remote_copy(
            src_ref=src,
            dst_ref=dst,
            send_sem=send_sem.at[number],
            recv_sem=recv_sem.at[number],
            device_id={"ctx": device},
            device_id_type=MESH,
        )

    def send(src, dst, device, goes=None, comes=None):
        copy = remote(src, dst, device)
        when(goes, copy.start)
        sent.append((copy, goes))
        return copy, comes

    def arrive(message):
        when(message[1], message[0].wait_recv)

    def head(number):
        return pl.ds(pl.multiple_of(number * BOX, BOX), BOX)

    third = BOX // 8
    for kind in range(2):
        loads[kind].wait()
        half1[kind] = pool(source[kind])
        far[kind] = pool(pool(half1[kind]))
    pl.semaphore_wait(barrier, ROWS - 1 + (z + zs - 1) // zs + (2 * zs - 2 - z) // zs)

    own_third = pl.ds(pl.multiple_of(3 * BOX + rank * third, third), third)
    own_half = pl.ds(pl.multiple_of(2 * BOX + rank * (BOX // 2), BOX // 2), BOX // 2)
    own_query = pl.ds(pl.multiple_of(rank * (BOX // 2), BOX // 2), BOX // 2)
    far_in = [
        send(far.at[:, :, head(ring(turn, flip))], kv3.at[:, own_third, :], z * ROWS + ring(turn, flip))
        for turn, flip in peers
    ]
    kv_in = {
        (turn, flip): send(
            half1.at[pl.ds(0, 2), :, head(ring(turn, flip))], kv1.at[:, own_half, :], z * ROWS + ring(turn, flip)
        )
        for turn, flip in peers
    }
    loads[2].wait()
    half1[2] = pool(source[2])
    q_in = [
        send(half1.at[2, :, head(ring(turn, flip))], q1.at[own_query, :], z * ROWS + ring(turn, flip))
        for turn, flip in peers
    ]
    last = rank // (ROWS - 1)
    at_end = (rank == 0) | (rank == ROWS - 1)
    towards = (last == 1) & has_right | (rank == 0) & has_left
    behind = (last == 1) & has_left | (rank == 0) & has_right
    relay_in = send(source.at[pl.ds(0, 2)], relay, column(z - 1 + 2 * last), towards, behind)

    kv3[:, own_third, :] = far[:, :, head(rank)]
    kv1[:, own_half, :] = half1[0:2, :, head(rank)]
    q1[own_query, :] = half1[2, :, head(rank)]

    def tell(turn):
        reach = 1 << turn
        when(z >= reach, lambda: signal(round_sem.at[turn], column(z - reach)))
        when(z < zs - reach, lambda: signal(round_sem.at[turn], column(z + reach)))

    def hear(turn):
        reach = 1 << turn
        pl.semaphore_wait(round_sem.at[turn], (z + zs - reach) // zs + (2 * zs - 1 - z - reach) // zs)

    tell(0)
    hear(0)
    tell(1)
    for message in far_in:
        arrive(message)
    own3 = kv3.at[:, pl.ds(3 * BOX, BOX), :]
    a_in = send(own3, kv3.at[:, pl.ds(0, BOX), :], column(z + 2), has_b, has_a)
    b_in = send(own3, kv3.at[:, pl.ds(BOX, BOX), :], column(z - 2), has_a, has_b)
    for kind in range(2):
        kv4[kind, 2 * BOX : 2 * BOX + BOX // 2, :] = pool(kv3[kind, 3 * BOX : 4 * BOX, :])
    hear(1)
    tell(2)
    own4 = kv4.at[:, pl.ds(2 * BOX, BOX // 2), :]
    half = pl.multiple_of(odd * (BOX // 2), BOX // 2)
    far4 = [
        (remote(own4, kv4.at[:, pl.ds(BOX + half, BOX // 2), :], column(mate(mirrored))), has_e),
        (remote(own4, kv4.at[:, pl.ds(BOX + half, BOX // 2), :], column(mirrored)), has_e),
        (remote(own4, kv4.at[:, pl.ds(half, BOX // 2), :], column(opposite)), z >= 0),
        (remote(own4, kv4.at[:, pl.ds(half, BOX // 2), :], column(mate(opposite))), z >= 0),
    ]
    sent.extend(far4)

    def send_far4(chosen):
        when(chosen, lambda: hear(2))
        for copy, goes in far4:
            when(chosen & goes, copy.start)

    send_far4(z >= zs // 2)
    near1 = []
    for turn in (0, 1, 3, 2):
        chip = lax.rem(y + turn, 4)
        back = (4 - turn) % 4
        for flip in range(2):
            if (back, flip) in kv_in:
                arrive(kv_in[back, flip])
        up = chip >= 2
        near1.append(
            send(
                kv1.at[:, head(2 + chip), :],
                kv1.at[:, head(lax.rem(chip + 6, 8)), :],
                column(z - 1 + 2 * (chip // 2)),
                (up & has_right) | (jnp.logical_not(up) & has_left),
                (up & has_left) | (jnp.logical_not(up) & has_right),
            )
        )
    for kind in range(2):
        for n in range(2):
            kv2[kind, (2 + n) * BOX : (3 + n) * BOX, :] = pool(kv1[kind, (2 * n + 2) * BOX : (2 * n + 4) * BOX, :])
    left2 = send(kv2.at[:, pl.ds(2 * BOX, BOX), :], kv2.at[:, pl.ds(0, BOX), :], column(z + 1), has_right, has_left)
    right2 = send(kv2.at[:, pl.ds(3 * BOX, BOX), :], kv2.at[:, pl.ds(5 * BOX, BOX), :], column(z - 1), has_left, has_right)

    send_far4(z < zs // 2)

    right0 = send(source.at[pl.ds(0, 2)], near.at[0], me + 1, rank < ROWS - 1, rank > 0)
    left0 = send(source.at[pl.ds(0, 2)], near.at[1], me - 1, rank > 0, rank < ROWS - 1)
    arrive(relay_in)
    around0 = send(relay, near.at[1 - last], z * ROWS + ROWS - 1 - rank, behind, towards)

    arrive(a_in)
    arrive(b_in)
    c_in = send(
        kv3.at[:, head(odd), :],
        kv3.at[:, pl.ds(2 * BOX, BOX), :],
        column(mate(z)),
        ((odd == 0) & has_a) | ((odd == 1) & has_b),
        has_c,
    )

    def bias(present):
        return jnp.where(present, 0.0, MASKED).astype(jnp.float32)

    left_bias, right_bias = bias(has_left), bias(has_right)

    for message in q_in:
        arrive(message)
    for n in range(2):
        q2[n * BOX : (n + 1) * BOX, :] = pool(q1[2 * n * BOX : (2 * n + 2) * BOX, :])
    q3 = pool(q2[...])
    q4 = pool(q3)

    def box(ref, kind, start):
        return ref[kind, start * BOX : (start + 1) * BOX, :]

    def level(query, ref, boxes, biases):
        return attend(query, [box(ref, 0, b) for b in boxes], [box(ref, 1, b) for b in boxes], biases)

    def raised(values, height):
        return values[0] + float(height), values[1], values[2]

    def repeated(values, start, times):
        count = values[0].shape[0]
        for kind in range(3):
            for turn in range(times):
                ups[kind, pl.ds(start + turn, count, times), :] = values[kind]

    def risen(start, count):
        return tuple(ups[kind, start : start + count, :] for kind in range(3))

    for message in near1:
        arrive(message)
    for kind in range(2):
        kv2[kind, BOX : 2 * BOX, :] = pool(kv1[kind, 0 : 2 * BOX, :])
        kv2[kind, 4 * BOX : 5 * BOX, :] = pool(kv1[kind, 6 * BOX : 8 * BOX, :])
    level1 = []
    for n, boxes in enumerate(((0, 4, 5), (1, 5, 0), (2, 6, 7), (3, 7, 2))):
        biases = [left_bias if b < 2 else right_bias if b >= 6 else None for b in boxes]
        level1.append(raised(level(q1[n * BOX : (n + 1) * BOX, :], kv1, boxes, biases), 1))
    arrive(left2)
    arrive(right2)
    for n, boxes in enumerate(((0, 4, 5), (1, 5, 0))):
        biases = [left_bias if b < 2 else right_bias for b in boxes]
        level2 = raised(level(q2[n * BOX : (n + 1) * BOX, :], kv2, boxes, biases), 2)
        repeated(level2, 2 * n * BOX, 2)
        for m in range(2):
            merged = merge(level1[2 * n + m], risen((2 * n + m) * BOX, BOX))
            for kind in range(3):
                terms[kind, (2 * n + m) * BOX : (2 * n + m + 1) * BOX, :] = merged[kind]

    arrive(c_in)
    level3 = raised(level(q3, kv3, (0, 1, 2), [bias(has_a), bias(has_b), bias(has_c)]), 3)
    for message in far4:
        arrive(message)
    repeated(raised(level(q4, kv4, (0, 1), [None, bias(has_e)]), 4), 0, 2)
    repeated(merge(level3, risen(0, BOX)), 4 * BOX, 4)

    here = lax.broadcasted_iota(jnp.int32, (BOX // 2, BOX), 0) == lax.broadcasted_iota(jnp.int32, (BOX // 2, BOX), 1)
    line = lax.broadcasted_iota(jnp.int32, (16, BOX), 0)

    def finish(number, box_out):
        rows = pl.ds(pl.multiple_of(number * (BOX // 2), BOX // 2), BOX // 2)
        rows_up = pl.ds(pl.multiple_of(4 * BOX + number * (BOX // 2), BOX // 2), BOX // 2)
        peak, total, numerator = merge(
            tuple(terms[kind, rows, :] for kind in range(3)), tuple(ups[kind, rows_up, :] for kind in range(3))
        )
        box_out[0 : BOX // 2, :] = (numerator / total).astype(jnp.bfloat16)
        weight = jnp.sum(jnp.where(here, peak + jnp.log2(total), 0.0), axis=0, keepdims=True)
        high = weight.astype(jnp.bfloat16).astype(jnp.float32)
        middle = (weight - high).astype(jnp.bfloat16).astype(jnp.float32)
        parts = jnp.where(line == 0, high, jnp.where(line == 1, middle, weight - high - middle))
        box_out[BOX // 2 :, :] = jnp.where(line < 3, parts, 0.0).astype(jnp.bfloat16)

    home = {}
    for n, (turn, flip) in enumerate(peers):
        finish(ring(turn, flip), parcel.at[n])
        home[turn, flip] = send(parcel.at[n], inbox.at[rank], z * ROWS + ring(turn, flip))
    finish(rank, inbox.at[rank])

    arrive(right0)
    arrive(left0)
    arrive(around0)
    start_bias, end_bias = bias(jnp.logical_not(starts)), bias(jnp.logical_not(ends))
    for n in range(HEADS):
        columns = slice(n * BOX, (n + 1) * BOX)
        values = attend(
            source[2, :, columns],
            [near[0, 0, :, columns], source[0, :, columns], near[1, 0, :, columns]],
            [near[0, 1, :, columns], source[1, :, columns], near[1, 1, :, columns]],
            [start_bias, None, end_bias],
        )
        for kind in range(3):
            terms[kind, n * BOX : (n + 1) * BOX, :] = values[kind]

    for n, (turn, flip) in enumerate([(0, 0)] + peers[::-1]):
        if n:
            arrive(home[turn, flip])
        number = ring((4 - turn) % 4, flip)
        got = inbox.at[number]
        parts = got[BOX // 2 :, :].astype(jnp.float32)
        weight = parts[0:1, :] + parts[1:2, :] + parts[2:3, :]
        weight = jnp.sum(jnp.where(here, weight, 0.0), axis=1, keepdims=True)
        coarse = got[0 : BOX // 2, :].astype(jnp.float32)
        repeated((jnp.broadcast_to(weight, coarse.shape), jnp.ones_like(coarse), coarse), n * BOX, 2)
        fine = tuple(terms[kind, head(number), :] for kind in range(3))
        _, total, numerator = merge(fine, risen(n * BOX, BOX))
        out_ref[:, head(number)] = (numerator / total).astype(jnp.bfloat16)
    for copy, goes in sent:
        when(goes, copy.wait_send)


MESSAGES = 4 * (ROWS - 1) + 17


def solution(mesh):
    zs = mesh.shape["ctx"] // ROWS

    def step(q, k, v):
        anywhere = pl.BlockSpec(memory_space=pl.ANY)
        return pl.pallas_call(
            functools.partial(kernel, zs),
            out_shape=pltpu.VMEM(q.shape, jnp.bfloat16),
            in_specs=[anywhere] * 3,
            out_specs=pl.BlockSpec(memory_space=pltpu.VMEM),
            scratch_shapes=[
                pltpu.VMEM((3, BOX, HEADS * BOX), jnp.bfloat16),
                pltpu.VMEM((3, BOX // 2, HEADS * BOX), jnp.bfloat16),
                pltpu.VMEM((2, BOX // 8, HEADS * BOX), jnp.bfloat16),
                pltpu.VMEM((2, 2, BOX, HEADS * BOX), jnp.bfloat16),
                pltpu.VMEM((2, BOX, HEADS * BOX), jnp.bfloat16),
                pltpu.VMEM((4 * BOX, BOX), jnp.bfloat16),
                pltpu.VMEM((2 * BOX, BOX), jnp.bfloat16),
                pltpu.VMEM((2, 8 * BOX, BOX), jnp.bfloat16),
                pltpu.VMEM((2, 6 * BOX, BOX), jnp.bfloat16),
                pltpu.VMEM((2, 4 * BOX, BOX), jnp.bfloat16),
                pltpu.VMEM((2, 5 * BOX // 2, BOX), jnp.bfloat16),
                pltpu.VMEM((3, 8 * BOX, BOX), jnp.float32),
                pltpu.VMEM((3, 8 * BOX, BOX), jnp.float32),
                pltpu.VMEM((ROWS - 1, BOX // 2 + 16, BOX), jnp.bfloat16),
                pltpu.VMEM((ROWS, BOX // 2 + 16, BOX), jnp.bfloat16),
                pltpu.SemaphoreType.DMA((3,)),
                pltpu.SemaphoreType.DMA((MESSAGES,)),
                pltpu.SemaphoreType.DMA((MESSAGES,)),
                pltpu.SemaphoreType.REGULAR((3,)),
            ],
            compiler_params=pltpu.CompilerParams(
                collective_id=0, has_side_effects=True, vmem_limit_bytes=32 * 2**20
            ),
            cost_estimate=pl.CostEstimate(flops=400_000_000, bytes_accessed=2**20, transcendentals=800_000),
            name="attention",
        )(*(pltpu.with_memory_space_constraint(x, pltpu.HBM) for x in (q, k, v)))

    spec = P(("doc", "ctx"), None)
    return jax.shard_map(step, mesh=mesh, in_specs=(spec,) * 3, out_specs=spec, check_vma=False)
```

```python
import functools
import math

import jax
import jax.numpy as jnp
from jax import lax
from jax.experimental import pallas as pl
from jax.experimental.pallas import tpu as pltpu
from jax.sharding import PartitionSpec as P

MESH = pl.DeviceIdType.MESH
HEADS = 8
BOX = 128
ROWS = 8
MASKED = -1e30
TO_LOG2 = math.log2(math.e) / math.sqrt(128.0)


def pool(rows):
    count = rows.shape[0]
    target = lax.broadcasted_iota(jnp.int32, (count // 2, count), 0)
    source = lax.broadcasted_iota(jnp.int32, (count // 2, count), 1)
    pairs = jnp.where(source // 2 == target, 0.5, 0.0).astype(jnp.bfloat16)
    return jnp.dot(pairs, rows, preferred_element_type=jnp.float32).astype(jnp.bfloat16)


def attend(query, keys, values, biases):
    scores = []
    for key, bias in zip(keys, biases):
        score = lax.dot_general(query, key, (((1,), (1,)), ((), ())), preferred_element_type=jnp.float32) * TO_LOG2
        scores.append(score if bias is None else score + bias)
    peak = jnp.max(functools.reduce(jnp.maximum, scores), axis=1, keepdims=True)
    shifted = [jnp.exp2(score - peak) for score in scores]
    total = jnp.sum(functools.reduce(jnp.add, shifted), axis=1, keepdims=True)
    weights = jnp.concatenate([part.astype(jnp.bfloat16) for part in shifted], axis=1)
    numerator = jnp.dot(weights, jnp.concatenate(values, axis=0), preferred_element_type=jnp.float32)
    return jnp.broadcast_to(peak, numerator.shape), jnp.broadcast_to(total, numerator.shape), numerator


def merge(one, other):
    newest = jnp.maximum(one[0], other[0])
    keep_one = jnp.exp2(one[0] - newest)
    keep_other = jnp.exp2(other[0] - newest)
    return newest, one[1] * keep_one + other[1] * keep_other, one[2] * keep_one + other[2] * keep_other


def kernel(zs, q_hbm, k_hbm, v_hbm, out_ref, source, half1, far, near, relay, q1, q2, kv1, kv2, kv3, kv4, terms, ups, parcel, inbox, load_sem, send_sem, recv_sem, round_sem):
    me = lax.axis_index("ctx")
    z = me // ROWS
    rank = lax.rem(me, ROWS)
    y, core = rank // 2, lax.rem(rank, 2)
    odd = lax.rem(z, 2)

    def ring(turn, flip):
        return 2 * lax.rem(y + turn, 4) + lax.rem(core + flip, 2)

    def column(other):
        return lax.rem(other + zs, zs) * ROWS + rank

    def mate(other):
        return other + 1 - 2 * lax.rem(other, 2)

    peers = [(2, 0), (2, 1), (1, 0), (1, 1), (3, 0), (3, 1), (0, 1)]
    opposite = lax.rem(z + zs // 2, zs)
    mirrored = zs - 1 - z
    has_left = z > 0
    has_right = z < zs - 1
    has_a = z >= 2
    has_b = z < zs - 2
    has_c = ((odd == 0) & (z + 3 < zs)) | ((odd == 1) & (z >= 3))
    has_e = (z < 2) | (z >= zs - 2)

    loads = [
        pltpu.make_async_copy(ref, source.at[n], load_sem.at[n]) for n, ref in enumerate((k_hbm, v_hbm, q_hbm))
    ]
    for load in loads:
        load.start()

    def when(present, action):
        if present is None:
            action()
        else:
            pl.when(present)(action)

    def signal(semaphore, device):
        pl.semaphore_signal(semaphore, inc=1, device_id={"ctx": device}, device_id_type=MESH)

    barrier = pltpu.get_barrier_semaphore()
    for turn, flip in peers:
        signal(barrier, z * ROWS + ring(turn, flip))
    when(has_left, lambda: signal(barrier, column(z - 1)))
    when(has_right, lambda: signal(barrier, column(z + 1)))

    def blank(ref, present, start, count):
        @pl.when(jnp.logical_not(present))
        def _():
            ref[:, start : start + count, :] = jnp.zeros((2, count, BOX), jnp.bfloat16)

    blank(kv1, has_left, 0, 2 * BOX)
    blank(kv1, has_right, 6 * BOX, 2 * BOX)
    blank(kv2, has_left, 0, BOX)
    blank(kv2, has_right, 5 * BOX, BOX)
    blank(kv3, has_a, 0, BOX)
    blank(kv3, has_b, BOX, BOX)
    blank(kv3, has_c, 2 * BOX, BOX)
    blank(kv4, has_e, BOX, BOX)

    starts = (z == 0) & (rank == 0)
    ends = (z == zs - 1) & (rank == ROWS - 1)

    @pl.when(starts)
    def _():
        near[0] = jnp.zeros(near.shape[1:], jnp.bfloat16)

    @pl.when(ends)
    def _():
        near[1] = jnp.zeros(near.shape[1:], jnp.bfloat16)

    used = [0]
    sent = []

    def remote(src, dst, device):
        number = used[0]
        used[0] += 1
        return pltpu.make_async_remote_copy(
            src_ref=src,
            dst_ref=dst,
            send_sem=send_sem.at[number],
            recv_sem=recv_sem.at[number],
            device_id={"ctx": device},
            device_id_type=MESH,
        )

    def send(src, dst, device, goes=None, comes=None):
        copy = remote(src, dst, device)
        when(goes, copy.start)
        sent.append((copy, goes))
        return copy, comes

    def arrive(message):
        when(message[1], message[0].wait_recv)

    def head(number):
        return pl.ds(pl.multiple_of(number * BOX, BOX), BOX)

    third = BOX // 8
    for kind in range(2):
        loads[kind].wait()
        half1[kind] = pool(source[kind])
        far[kind] = pool(pool(half1[kind]))
    pl.semaphore_wait(barrier, ROWS - 1 + (z + zs - 1) // zs + (2 * zs - 2 - z) // zs)

    upward, downward, everyone = (round_sem.at[n] for n in range(3))
    when(has_left, lambda: signal(downward, column(z - 1)))

    own_third = pl.ds(pl.multiple_of(3 * BOX + rank * third, third), third)
    own_half = pl.ds(pl.multiple_of(2 * BOX + rank * (BOX // 2), BOX // 2), BOX // 2)
    own_query = pl.ds(pl.multiple_of(rank * (BOX // 2), BOX // 2), BOX // 2)
    far_in = [
        send(far.at[:, :, head(ring(turn, flip))], kv3.at[:, own_third, :], z * ROWS + ring(turn, flip))
        for turn, flip in peers
    ]
    kv_in = {
        (turn, flip): send(
            half1.at[pl.ds(0, 2), :, head(ring(turn, flip))], kv1.at[:, own_half, :], z * ROWS + ring(turn, flip)
        )
        for turn, flip in peers
    }
    loads[2].wait()
    half1[2] = pool(source[2])
    q_in = [
        send(half1.at[2, :, head(ring(turn, flip))], q1.at[own_query, :], z * ROWS + ring(turn, flip))
        for turn, flip in peers
    ]
    last = rank // (ROWS - 1)
    at_end = (rank == 0) | (rank == ROWS - 1)
    towards = (last == 1) & has_right | (rank == 0) & has_left
    behind = (last == 1) & has_left | (rank == 0) & has_right
    beyond = column(z - 1 + 2 * last)
    before = column(z + 1 - 2 * last)
    other_end = z * ROWS + ROWS - 1 - rank
    relay_keys = send(source.at[0], relay.at[0], beyond, towards, behind)

    when(has_left, lambda: pl.semaphore_wait(upward, 1))
    when(has_right, lambda: signal(upward, column(z + 1)))
    for other in range(zs // 2):
        when(z == zs - 1, lambda: signal(everyone, column(other)))

    kv3[:, own_third, :] = far[:, :, head(rank)]
    kv1[:, own_half, :] = half1[0:2, :, head(rank)]
    q1[own_query, :] = half1[2, :, head(rank)]

    near1 = []

    def send_box1(turn):
        chip = lax.rem(y + turn, 4)
        for flip in range(2):
            if ((4 - turn) % 4, flip) in kv_in:
                arrive(kv_in[(4 - turn) % 4, flip])
        up = chip >= 2
        near1.append(
            send(
                kv1.at[:, head(2 + chip), :],
                kv1.at[:, head(lax.rem(chip + 6, 8)), :],
                column(z - 1 + 2 * (chip // 2)),
                (up & has_right) | (jnp.logical_not(up) & has_left),
                (up & has_left) | (jnp.logical_not(up) & has_right),
            )
        )

    send_box1(0)
    when(has_right, lambda: pl.semaphore_wait(downward, 1))
    for message in far_in:
        arrive(message)
    own3 = kv3.at[:, pl.ds(3 * BOX, BOX), :]
    a_in = send(own3, kv3.at[:, pl.ds(0, BOX), :], column(z + 2), has_b, has_a)
    b_in = send(own3, kv3.at[:, pl.ds(BOX, BOX), :], column(z - 2), has_a, has_b)
    for kind in range(2):
        kv4[kind, 2 * BOX : 2 * BOX + BOX // 2, :] = pool(kv3[kind, 3 * BOX : 4 * BOX, :])
    own4 = kv4.at[:, pl.ds(2 * BOX, BOX // 2), :]
    half = pl.multiple_of(odd * (BOX // 2), BOX // 2)
    far4 = [
        (remote(own4, kv4.at[:, pl.ds(BOX + half, BOX // 2), :], column(mate(mirrored))), has_e),
        (remote(own4, kv4.at[:, pl.ds(BOX + half, BOX // 2), :], column(mirrored)), has_e),
        (remote(own4, kv4.at[:, pl.ds(half, BOX // 2), :], column(opposite)), z >= 0),
        (remote(own4, kv4.at[:, pl.ds(half, BOX // 2), :], column(mate(opposite))), z >= 0),
    ]
    sent.extend(far4)

    def send_far4(chosen):
        for copy, goes in far4:
            when(chosen & goes, copy.start)

    send_far4(z >= zs // 2)
    for turn in (1, 3, 2):
        send_box1(turn)
    for kind in range(2):
        for n in range(2):
            kv2[kind, (2 + n) * BOX : (3 + n) * BOX, :] = pool(kv1[kind, (2 * n + 2) * BOX : (2 * n + 4) * BOX, :])
    left2 = send(kv2.at[:, pl.ds(2 * BOX, BOX), :], kv2.at[:, pl.ds(0, BOX), :], column(z + 1), has_right, has_left)
    right2 = send(kv2.at[:, pl.ds(3 * BOX, BOX), :], kv2.at[:, pl.ds(5 * BOX, BOX), :], column(z - 1), has_left, has_right)

    relay_values = send(source.at[1], relay.at[1], other_end, towards, behind)
    right0 = send(source.at[pl.ds(0, 2)], near.at[0], me + 1, rank < ROWS - 1, rank > 0)
    left0 = send(source.at[pl.ds(0, 2)], near.at[1], me - 1, rank > 0, rank < ROWS - 1)

    arrive(relay_keys)
    around_keys = send(relay.at[0], near.at[1 - last, 0], other_end, behind, towards)
    arrive(a_in)
    arrive(b_in)
    c_in = send(
        kv3.at[:, head(odd), :],
        kv3.at[:, pl.ds(2 * BOX, BOX), :],
        column(mate(z)),
        ((odd == 0) & has_a) | ((odd == 1) & has_b),
        has_c,
    )

    when(z < zs // 2, lambda: pl.semaphore_wait(everyone, 1))
    send_far4(z < zs // 2)

    def bias(present):
        return jnp.where(present, 0.0, MASKED).astype(jnp.float32)

    left_bias, right_bias = bias(has_left), bias(has_right)

    arrive(relay_values)
    around_values = send(relay.at[1], near.at[last, 1], before, behind, towards)
    for message in q_in:
        arrive(message)
    for n in range(2):
        q2[n * BOX : (n + 1) * BOX, :] = pool(q1[2 * n * BOX : (2 * n + 2) * BOX, :])
    q3 = pool(q2[...])
    q4 = pool(q3)


    def box(ref, kind, start):
        return ref[kind, start * BOX : (start + 1) * BOX, :]

    def level(query, ref, boxes, biases):
        return attend(query, [box(ref, 0, b) for b in boxes], [box(ref, 1, b) for b in boxes], biases)

    def raised(values, height):
        return values[0] + float(height), values[1], values[2]

    def repeated(values, start, times):
        count = values[0].shape[0]
        for kind in range(3):
            for turn in range(times):
                ups[kind, pl.ds(start + turn, count, times), :] = values[kind]

    def risen(start, count):
        return tuple(ups[kind, start : start + count, :] for kind in range(3))

    for message in near1:
        arrive(message)
    for kind in range(2):
        kv2[kind, BOX : 2 * BOX, :] = pool(kv1[kind, 0 : 2 * BOX, :])
        kv2[kind, 4 * BOX : 5 * BOX, :] = pool(kv1[kind, 6 * BOX : 8 * BOX, :])
    level1 = []
    for n, boxes in enumerate(((0, 4, 5), (1, 5, 0), (2, 6, 7), (3, 7, 2))):
        biases = [left_bias if b < 2 else right_bias if b >= 6 else None for b in boxes]
        level1.append(raised(level(q1[n * BOX : (n + 1) * BOX, :], kv1, boxes, biases), 1))
    arrive(left2)
    arrive(right2)
    for n, boxes in enumerate(((0, 4, 5), (1, 5, 0))):
        biases = [left_bias if b < 2 else right_bias for b in boxes]
        level2 = raised(level(q2[n * BOX : (n + 1) * BOX, :], kv2, boxes, biases), 2)
        repeated(level2, 2 * n * BOX, 2)
        for m in range(2):
            merged = merge(level1[2 * n + m], risen((2 * n + m) * BOX, BOX))
            for kind in range(3):
                terms[kind, (2 * n + m) * BOX : (2 * n + m + 1) * BOX, :] = merged[kind]

    arrive(c_in)
    level3 = raised(level(q3, kv3, (0, 1, 2), [bias(has_a), bias(has_b), bias(has_c)]), 3)
    for message in far4:
        arrive(message)
    repeated(raised(level(q4, kv4, (0, 1), [None, bias(has_e)]), 4), 0, 2)
    repeated(merge(level3, risen(0, BOX)), 4 * BOX, 4)

    here = lax.broadcasted_iota(jnp.int32, (BOX // 2, BOX), 0) == lax.broadcasted_iota(jnp.int32, (BOX // 2, BOX), 1)
    line = lax.broadcasted_iota(jnp.int32, (16, BOX), 0)

    def finish(number, box_out):
        rows = pl.ds(pl.multiple_of(number * (BOX // 2), BOX // 2), BOX // 2)
        rows_up = pl.ds(pl.multiple_of(4 * BOX + number * (BOX // 2), BOX // 2), BOX // 2)
        peak, total, numerator = merge(
            tuple(terms[kind, rows, :] for kind in range(3)), tuple(ups[kind, rows_up, :] for kind in range(3))
        )
        box_out[0 : BOX // 2, :] = (numerator / total).astype(jnp.bfloat16)
        weight = jnp.sum(jnp.where(here, peak + jnp.log2(total), 0.0), axis=0, keepdims=True)
        high = weight.astype(jnp.bfloat16).astype(jnp.float32)
        middle = (weight - high).astype(jnp.bfloat16).astype(jnp.float32)
        parts = jnp.where(line == 0, high, jnp.where(line == 1, middle, weight - high - middle))
        box_out[BOX // 2 :, :] = jnp.where(line < 3, parts, 0.0).astype(jnp.bfloat16)

    home = {}
    for n, (turn, flip) in enumerate(peers):
        finish(ring(turn, flip), parcel.at[n])
        home[turn, flip] = send(parcel.at[n], inbox.at[rank], z * ROWS + ring(turn, flip))
    finish(rank, inbox.at[rank])

    arrive(right0)
    arrive(left0)
    arrive(around_keys)
    arrive(around_values)
    start_bias, end_bias = bias(jnp.logical_not(starts)), bias(jnp.logical_not(ends))
    for n in range(HEADS):
        columns = slice(n * BOX, (n + 1) * BOX)
        values = attend(
            source[2, :, columns],
            [near[0, 0, :, columns], source[0, :, columns], near[1, 0, :, columns]],
            [near[0, 1, :, columns], source[1, :, columns], near[1, 1, :, columns]],
            [start_bias, None, end_bias],
        )
        for kind in range(3):
            terms[kind, n * BOX : (n + 1) * BOX, :] = values[kind]

    for n, (turn, flip) in enumerate([(0, 0)] + peers[::-1]):
        if n:
            arrive(home[turn, flip])
        number = ring((4 - turn) % 4, flip)
        got = inbox.at[number]
        parts = got[BOX // 2 :, :].astype(jnp.float32)
        weight = parts[0:1, :] + parts[1:2, :] + parts[2:3, :]
        weight = jnp.sum(jnp.where(here, weight, 0.0), axis=1, keepdims=True)
        coarse = got[0 : BOX // 2, :].astype(jnp.float32)
        repeated((jnp.broadcast_to(weight, coarse.shape), jnp.ones_like(coarse), coarse), n * BOX, 2)
        fine = tuple(terms[kind, head(number), :] for kind in range(3))
        _, total, numerator = merge(fine, risen(n * BOX, BOX))
        out_ref[:, head(number)] = (numerator / total).astype(jnp.bfloat16)
    for copy, goes in sent:
        when(goes, copy.wait_send)


MESSAGES = 4 * (ROWS - 1) + 19


def solution(mesh):
    zs = mesh.shape["ctx"] // ROWS

    def step(q, k, v):
        anywhere = pl.BlockSpec(memory_space=pl.ANY)
        return pl.pallas_call(
            functools.partial(kernel, zs),
            out_shape=pltpu.VMEM(q.shape, jnp.bfloat16),
            in_specs=[anywhere] * 3,
            out_specs=pl.BlockSpec(memory_space=pltpu.VMEM),
            scratch_shapes=[
                pltpu.VMEM((3, BOX, HEADS * BOX), jnp.bfloat16),
                pltpu.VMEM((3, BOX // 2, HEADS * BOX), jnp.bfloat16),
                pltpu.VMEM((2, BOX // 8, HEADS * BOX), jnp.bfloat16),
                pltpu.VMEM((2, 2, BOX, HEADS * BOX), jnp.bfloat16),
                pltpu.VMEM((2, BOX, HEADS * BOX), jnp.bfloat16),
                pltpu.VMEM((4 * BOX, BOX), jnp.bfloat16),
                pltpu.VMEM((2 * BOX, BOX), jnp.bfloat16),
                pltpu.VMEM((2, 8 * BOX, BOX), jnp.bfloat16),
                pltpu.VMEM((2, 6 * BOX, BOX), jnp.bfloat16),
                pltpu.VMEM((2, 4 * BOX, BOX), jnp.bfloat16),
                pltpu.VMEM((2, 5 * BOX // 2, BOX), jnp.bfloat16),
                pltpu.VMEM((3, 8 * BOX, BOX), jnp.float32),
                pltpu.VMEM((3, 8 * BOX, BOX), jnp.float32),
                pltpu.VMEM((ROWS - 1, BOX // 2 + 16, BOX), jnp.bfloat16),
                pltpu.VMEM((ROWS, BOX // 2 + 16, BOX), jnp.bfloat16),
                pltpu.SemaphoreType.DMA((3,)),
                pltpu.SemaphoreType.DMA((MESSAGES,)),
                pltpu.SemaphoreType.DMA((MESSAGES,)),
                pltpu.SemaphoreType.REGULAR((3,)),
            ],
            compiler_params=pltpu.CompilerParams(
                collective_id=0, has_side_effects=True, vmem_limit_bytes=32 * 2**20
            ),
            cost_estimate=pl.CostEstimate(flops=400_000_000, bytes_accessed=2**20, transcendentals=800_000),
            name="attention",
        )(*(pltpu.with_memory_space_constraint(x, pltpu.HBM) for x in (q, k, v)))

    spec = P(("doc", "ctx"), None)
    return jax.shard_map(step, mesh=mesh, in_specs=(spec,) * 3, out_specs=spec, check_vma=False)
```

```python
import functools
import math

import jax
import jax.numpy as jnp
from jax import lax
from jax.experimental import pallas as pl
from jax.experimental.pallas import tpu as pltpu
from jax.sharding import PartitionSpec as P

MESH = pl.DeviceIdType.MESH
HEADS = 8
BOX = 128
ROWS = 8
MASKED = -1e30
TO_LOG2 = math.log2(math.e) / math.sqrt(128.0)


def pool(rows):
    count = rows.shape[0]
    target = lax.broadcasted_iota(jnp.int32, (count // 2, count), 0)
    source = lax.broadcasted_iota(jnp.int32, (count // 2, count), 1)
    pairs = jnp.where(source // 2 == target, 0.5, 0.0).astype(jnp.bfloat16)
    return jnp.dot(pairs, rows, preferred_element_type=jnp.float32).astype(jnp.bfloat16)


def attend(query, keys, values, biases):
    scores = []
    for key, bias in zip(keys, biases):
        score = lax.dot_general(query, key, (((1,), (1,)), ((), ())), preferred_element_type=jnp.float32) * TO_LOG2
        scores.append(score if bias is None else score + bias)
    peak = jnp.max(functools.reduce(jnp.maximum, scores), axis=1, keepdims=True)
    shifted = [jnp.exp2(score - peak) for score in scores]
    total = jnp.sum(functools.reduce(jnp.add, shifted), axis=1, keepdims=True)
    weights = jnp.concatenate([part.astype(jnp.bfloat16) for part in shifted], axis=1)
    numerator = jnp.dot(weights, jnp.concatenate(values, axis=0), preferred_element_type=jnp.float32)
    return jnp.broadcast_to(peak, numerator.shape), jnp.broadcast_to(total, numerator.shape), numerator


def merge(one, other):
    newest = jnp.maximum(one[0], other[0])
    keep_one = jnp.exp2(one[0] - newest)
    keep_other = jnp.exp2(other[0] - newest)
    return newest, one[1] * keep_one + other[1] * keep_other, one[2] * keep_one + other[2] * keep_other


def kernel(zs, q_hbm, k_hbm, v_hbm, out_ref, source, half1, far, near, relay, q1, q2, kv1, kv2, kv3, kv4, terms, ups, parcel, inbox, load_sem, send_sem, recv_sem, round_sem):
    me = lax.axis_index("ctx")
    z = me // ROWS
    rank = lax.rem(me, ROWS)
    y, core = rank // 2, lax.rem(rank, 2)
    odd = lax.rem(z, 2)

    def ring(turn, flip):
        return 2 * lax.rem(y + turn, 4) + lax.rem(core + flip, 2)

    def column(other):
        return lax.rem(other + zs, zs) * ROWS + rank

    def mate(other):
        return other + 1 - 2 * lax.rem(other, 2)

    peers = [(2, 0), (2, 1), (1, 0), (1, 1), (3, 0), (3, 1), (0, 1)]
    opposite = lax.rem(z + zs // 2, zs)
    passed_on = (z == zs // 4) | (z == zs // 4 + 1)
    mirrored = zs - 1 - z
    has_left = z > 0
    has_right = z < zs - 1
    has_a = z >= 2
    has_b = z < zs - 2
    has_c = ((odd == 0) & (z + 3 < zs)) | ((odd == 1) & (z >= 3))
    has_e = (z < 2) | (z >= zs - 2)

    loads = [
        pltpu.make_async_copy(ref, source.at[n], load_sem.at[n]) for n, ref in enumerate((k_hbm, v_hbm, q_hbm))
    ]
    for load in loads:
        load.start()

    def when(present, action):
        if present is None:
            action()
        else:
            pl.when(present)(action)

    def signal(semaphore, device):
        pl.semaphore_signal(semaphore, inc=1, device_id={"ctx": device}, device_id_type=MESH)

    barrier = pltpu.get_barrier_semaphore()
    for turn, flip in peers:
        signal(barrier, z * ROWS + ring(turn, flip))
    when(has_left, lambda: signal(barrier, column(z - 1)))
    when(has_right, lambda: signal(barrier, column(z + 1)))

    def blank(ref, present, start, count):
        @pl.when(jnp.logical_not(present))
        def _():
            ref[:, start : start + count, :] = jnp.zeros((2, count, BOX), jnp.bfloat16)

    blank(kv1, has_left, 0, 2 * BOX)
    blank(kv1, has_right, 6 * BOX, 2 * BOX)
    blank(kv2, has_left, 0, BOX)
    blank(kv2, has_right, 5 * BOX, BOX)
    blank(kv3, has_a, 0, BOX)
    blank(kv3, has_b, BOX, BOX)
    blank(kv3, has_c, 2 * BOX, BOX)
    blank(kv4, has_e, BOX, BOX)

    starts = (z == 0) & (rank == 0)
    ends = (z == zs - 1) & (rank == ROWS - 1)

    @pl.when(starts)
    def _():
        near[0] = jnp.zeros(near.shape[1:], jnp.bfloat16)

    @pl.when(ends)
    def _():
        near[1] = jnp.zeros(near.shape[1:], jnp.bfloat16)

    used = [0]
    sent = []

    def remote(src, dst, device):
        number = used[0]
        used[0] += 1
        return pltpu.make_async_remote_copy(
            src_ref=src,
            dst_ref=dst,
            send_sem=send_sem.at[number],
            recv_sem=recv_sem.at[number],
            device_id={"ctx": device},
            device_id_type=MESH,
        )

    def send(src, dst, device, goes=None, comes=None):
        copy = remote(src, dst, device)
        when(goes, copy.start)
        sent.append((copy, goes))
        return copy, comes

    def arrive(message):
        when(message[1], message[0].wait_recv)

    def head(number):
        return pl.ds(pl.multiple_of(number * BOX, BOX), BOX)

    third = BOX // 8
    for kind in range(2):
        loads[kind].wait()
        half1[kind] = pool(source[kind])
        far[kind] = pool(pool(half1[kind]))
    pl.semaphore_wait(barrier, ROWS - 1 + (z + zs - 1) // zs + (2 * zs - 2 - z) // zs)

    upward, downward, everyone = (round_sem.at[n] for n in range(3))
    when(has_left, lambda: signal(downward, column(z - 1)))

    own_third = pl.ds(pl.multiple_of(3 * BOX + rank * third, third), third)
    own_half = pl.ds(pl.multiple_of(2 * BOX + rank * (BOX // 2), BOX // 2), BOX // 2)
    own_query = pl.ds(pl.multiple_of(rank * (BOX // 2), BOX // 2), BOX // 2)
    far_in = [
        send(far.at[:, :, head(ring(turn, flip))], kv3.at[:, own_third, :], z * ROWS + ring(turn, flip))
        for turn, flip in peers
    ]
    kv_in = {
        (turn, flip): send(
            half1.at[pl.ds(0, 2), :, head(ring(turn, flip))], kv1.at[:, own_half, :], z * ROWS + ring(turn, flip)
        )
        for turn, flip in peers
    }
    loads[2].wait()
    half1[2] = pool(source[2])
    q_in = [
        send(half1.at[2, :, head(ring(turn, flip))], q1.at[own_query, :], z * ROWS + ring(turn, flip))
        for turn, flip in peers
    ]
    last = rank // (ROWS - 1)
    at_end = (rank == 0) | (rank == ROWS - 1)
    towards = (last == 1) & has_right | (rank == 0) & has_left
    behind = (last == 1) & has_left | (rank == 0) & has_right
    beyond = column(z - 1 + 2 * last)
    before = column(z + 1 - 2 * last)
    other_end = z * ROWS + ROWS - 1 - rank
    relay_keys = send(source.at[0], relay.at[0], beyond, towards, behind)

    when(has_left, lambda: pl.semaphore_wait(upward, 1))
    when(has_right, lambda: signal(upward, column(z + 1)))
    for other in range(zs // 2):
        when(z == zs - 1, lambda: signal(everyone, column(other)))

    kv3[:, own_third, :] = far[:, :, head(rank)]
    kv1[:, own_half, :] = half1[0:2, :, head(rank)]
    q1[own_query, :] = half1[2, :, head(rank)]

    near1 = []

    def send_box1(turn):
        chip = lax.rem(y + turn, 4)
        for flip in range(2):
            if ((4 - turn) % 4, flip) in kv_in:
                arrive(kv_in[(4 - turn) % 4, flip])
        up = chip >= 2
        near1.append(
            send(
                kv1.at[:, head(2 + chip), :],
                kv1.at[:, head(lax.rem(chip + 6, 8)), :],
                column(z - 1 + 2 * (chip // 2)),
                (up & has_right) | (jnp.logical_not(up) & has_left),
                (up & has_left) | (jnp.logical_not(up) & has_right),
            )
        )

    send_box1(0)
    when(has_right, lambda: pl.semaphore_wait(downward, 1))
    for message in far_in:
        arrive(message)
    own3 = kv3.at[:, pl.ds(3 * BOX, BOX), :]
    a_in = send(own3, kv3.at[:, pl.ds(0, BOX), :], column(z + 2), has_b, has_a)
    b_in = send(own3, kv3.at[:, pl.ds(BOX, BOX), :], column(z - 2), has_a, has_b)
    for kind in range(2):
        kv4[kind, 2 * BOX : 2 * BOX + BOX // 2, :] = pool(kv3[kind, 3 * BOX : 4 * BOX, :])
    own4 = kv4.at[:, pl.ds(2 * BOX, BOX // 2), :]
    half = pl.multiple_of(odd * (BOX // 2), BOX // 2)
    far4 = [
        (remote(own4, kv4.at[:, pl.ds(BOX + half, BOX // 2), :], column(mate(mirrored))), has_e),
        (remote(own4, kv4.at[:, pl.ds(BOX + half, BOX // 2), :], column(mirrored)), has_e),
        (remote(own4, kv4.at[:, pl.ds(half, BOX // 2), :], column(opposite)), z < zs - 2),
        (remote(own4, kv4.at[:, pl.ds(half, BOX // 2), :], column(mate(opposite))), z >= 0),
    ]
    sent.extend(far4)

    def send_far4(chosen):
        for copy, goes in far4:
            when(chosen & goes, copy.start)

    send_far4(z >= zs // 2)
    for turn in (1, 3, 2):
        send_box1(turn)
    for kind in range(2):
        for n in range(2):
            kv2[kind, (2 + n) * BOX : (3 + n) * BOX, :] = pool(kv1[kind, (2 * n + 2) * BOX : (2 * n + 4) * BOX, :])
    left2 = send(kv2.at[:, pl.ds(2 * BOX, BOX), :], kv2.at[:, pl.ds(0, BOX), :], column(z + 1), has_right, has_left)
    right2 = send(kv2.at[:, pl.ds(3 * BOX, BOX), :], kv2.at[:, pl.ds(5 * BOX, BOX), :], column(z - 1), has_left, has_right)

    relay_values = send(source.at[1], relay.at[1], other_end, towards, behind)
    right0 = send(source.at[pl.ds(0, 2)], near.at[0], me + 1, rank < ROWS - 1, rank > 0)
    left0 = send(source.at[pl.ds(0, 2)], near.at[1], me - 1, rank > 0, rank < ROWS - 1)

    arrive(relay_keys)
    around_keys = send(relay.at[0], near.at[1 - last, 0], other_end, behind, towards)
    arrive(a_in)
    arrive(b_in)
    c_in = send(
        kv3.at[:, head(odd), :],
        kv3.at[:, pl.ds(2 * BOX, BOX), :],
        column(mate(z)),
        ((odd == 0) & has_a) | ((odd == 1) & has_b),
        has_c,
    )

    when(z < zs // 2, lambda: pl.semaphore_wait(everyone, 1))
    send_far4(z < zs // 2)

    def bias(present):
        return jnp.where(present, 0.0, MASKED).astype(jnp.float32)

    left_bias, right_bias = bias(has_left), bias(has_right)

    arrive(relay_values)
    around_values = send(relay.at[1], near.at[last, 1], before, behind, towards)
    for message in q_in:
        arrive(message)
    for n in range(2):
        q2[n * BOX : (n + 1) * BOX, :] = pool(q1[2 * n * BOX : (2 * n + 2) * BOX, :])
    q3 = pool(q2[...])
    q4 = pool(q3)


    def box(ref, kind, start):
        return ref[kind, start * BOX : (start + 1) * BOX, :]

    def level(query, ref, boxes, biases):
        return attend(query, [box(ref, 0, b) for b in boxes], [box(ref, 1, b) for b in boxes], biases)

    def raised(values, height):
        return values[0] + float(height), values[1], values[2]

    def repeated(values, start, times):
        count = values[0].shape[0]
        for kind in range(3):
            for turn in range(times):
                ups[kind, pl.ds(start + turn, count, times), :] = values[kind]

    def risen(start, count):
        return tuple(ups[kind, start : start + count, :] for kind in range(3))

    for message in near1:
        arrive(message)
    for kind in range(2):
        kv2[kind, BOX : 2 * BOX, :] = pool(kv1[kind, 0 : 2 * BOX, :])
        kv2[kind, 4 * BOX : 5 * BOX, :] = pool(kv1[kind, 6 * BOX : 8 * BOX, :])
    level1 = []
    for n, boxes in enumerate(((0, 4, 5), (1, 5, 0), (2, 6, 7), (3, 7, 2))):
        biases = [left_bias if b < 2 else right_bias if b >= 6 else None for b in boxes]
        level1.append(raised(level(q1[n * BOX : (n + 1) * BOX, :], kv1, boxes, biases), 1))
    arrive(far4[0])
    passed = send(
        kv4.at[:, pl.ds(pl.multiple_of(BOX + half, BOX // 2), BOX // 2), :],
        kv4.at[:, pl.ds(half, BOX // 2), :],
        column(z + 2),
        z < 2,
        passed_on,
    )

    arrive(left2)
    arrive(right2)
    for n, boxes in enumerate(((0, 4, 5), (1, 5, 0))):
        biases = [left_bias if b < 2 else right_bias for b in boxes]
        level2 = raised(level(q2[n * BOX : (n + 1) * BOX, :], kv2, boxes, biases), 2)
        repeated(level2, 2 * n * BOX, 2)
        for m in range(2):
            merged = merge(level1[2 * n + m], risen((2 * n + m) * BOX, BOX))
            for kind in range(3):
                terms[kind, (2 * n + m) * BOX : (2 * n + m + 1) * BOX, :] = merged[kind]

    arrive(c_in)
    level3 = raised(level(q3, kv3, (0, 1, 2), [bias(has_a), bias(has_b), bias(has_c)]), 3)
    arrive(far4[1])
    when(jnp.logical_not(passed_on), far4[2][0].wait_recv)
    arrive(passed)
    arrive(far4[3])
    repeated(raised(level(q4, kv4, (0, 1), [None, bias(has_e)]), 4), 0, 2)
    repeated(merge(level3, risen(0, BOX)), 4 * BOX, 4)

    here = lax.broadcasted_iota(jnp.int32, (BOX // 2, BOX), 0) == lax.broadcasted_iota(jnp.int32, (BOX // 2, BOX), 1)
    line = lax.broadcasted_iota(jnp.int32, (16, BOX), 0)

    def finish(number, box_out):
        rows = pl.ds(pl.multiple_of(number * (BOX // 2), BOX // 2), BOX // 2)
        rows_up = pl.ds(pl.multiple_of(4 * BOX + number * (BOX // 2), BOX // 2), BOX // 2)
        peak, total, numerator = merge(
            tuple(terms[kind, rows, :] for kind in range(3)), tuple(ups[kind, rows_up, :] for kind in range(3))
        )
        box_out[0 : BOX // 2, :] = (numerator / total).astype(jnp.bfloat16)
        weight = jnp.sum(jnp.where(here, peak + jnp.log2(total), 0.0), axis=0, keepdims=True)
        high = weight.astype(jnp.bfloat16).astype(jnp.float32)
        middle = (weight - high).astype(jnp.bfloat16).astype(jnp.float32)
        parts = jnp.where(line == 0, high, jnp.where(line == 1, middle, weight - high - middle))
        box_out[BOX // 2 :, :] = jnp.where(line < 3, parts, 0.0).astype(jnp.bfloat16)

    home = {}
    for n, (turn, flip) in enumerate(peers):
        finish(ring(turn, flip), parcel.at[n])
        home[turn, flip] = send(parcel.at[n], inbox.at[rank], z * ROWS + ring(turn, flip))
    finish(rank, inbox.at[rank])

    arrive(right0)
    arrive(left0)
    arrive(around_keys)
    arrive(around_values)
    start_bias, end_bias = bias(jnp.logical_not(starts)), bias(jnp.logical_not(ends))
    for n in range(HEADS):
        columns = slice(n * BOX, (n + 1) * BOX)
        values = attend(
            source[2, :, columns],
            [near[0, 0, :, columns], source[0, :, columns], near[1, 0, :, columns]],
            [near[0, 1, :, columns], source[1, :, columns], near[1, 1, :, columns]],
            [start_bias, None, end_bias],
        )
        for kind in range(3):
            terms[kind, n * BOX : (n + 1) * BOX, :] = values[kind]

    for n, (turn, flip) in enumerate([(0, 0)] + peers[::-1]):
        if n:
            arrive(home[turn, flip])
        number = ring((4 - turn) % 4, flip)
        got = inbox.at[number]
        parts = got[BOX // 2 :, :].astype(jnp.float32)
        weight = parts[0:1, :] + parts[1:2, :] + parts[2:3, :]
        weight = jnp.sum(jnp.where(here, weight, 0.0), axis=1, keepdims=True)
        coarse = got[0 : BOX // 2, :].astype(jnp.float32)
        repeated((jnp.broadcast_to(weight, coarse.shape), jnp.ones_like(coarse), coarse), n * BOX, 2)
        fine = tuple(terms[kind, head(number), :] for kind in range(3))
        _, total, numerator = merge(fine, risen(n * BOX, BOX))
        out_ref[:, head(number)] = (numerator / total).astype(jnp.bfloat16)
    for copy, goes in sent:
        when(goes, copy.wait_send)


MESSAGES = 4 * (ROWS - 1) + 20


def solution(mesh):
    zs = mesh.shape["ctx"] // ROWS

    def step(q, k, v):
        anywhere = pl.BlockSpec(memory_space=pl.ANY)
        return pl.pallas_call(
            functools.partial(kernel, zs),
            out_shape=pltpu.VMEM(q.shape, jnp.bfloat16),
            in_specs=[anywhere] * 3,
            out_specs=pl.BlockSpec(memory_space=pltpu.VMEM),
            scratch_shapes=[
                pltpu.VMEM((3, BOX, HEADS * BOX), jnp.bfloat16),
                pltpu.VMEM((3, BOX // 2, HEADS * BOX), jnp.bfloat16),
                pltpu.VMEM((2, BOX // 8, HEADS * BOX), jnp.bfloat16),
                pltpu.VMEM((2, 2, BOX, HEADS * BOX), jnp.bfloat16),
                pltpu.VMEM((2, BOX, HEADS * BOX), jnp.bfloat16),
                pltpu.VMEM((4 * BOX, BOX), jnp.bfloat16),
                pltpu.VMEM((2 * BOX, BOX), jnp.bfloat16),
                pltpu.VMEM((2, 8 * BOX, BOX), jnp.bfloat16),
                pltpu.VMEM((2, 6 * BOX, BOX), jnp.bfloat16),
                pltpu.VMEM((2, 4 * BOX, BOX), jnp.bfloat16),
                pltpu.VMEM((2, 5 * BOX // 2, BOX), jnp.bfloat16),
                pltpu.VMEM((3, 8 * BOX, BOX), jnp.float32),
                pltpu.VMEM((3, 8 * BOX, BOX), jnp.float32),
                pltpu.VMEM((ROWS - 1, BOX // 2 + 16, BOX), jnp.bfloat16),
                pltpu.VMEM((ROWS, BOX // 2 + 16, BOX), jnp.bfloat16),
                pltpu.SemaphoreType.DMA((3,)),
                pltpu.SemaphoreType.DMA((MESSAGES,)),
                pltpu.SemaphoreType.DMA((MESSAGES,)),
                pltpu.SemaphoreType.REGULAR((3,)),
            ],
            compiler_params=pltpu.CompilerParams(
                collective_id=0, has_side_effects=True, vmem_limit_bytes=32 * 2**20
            ),
            cost_estimate=pl.CostEstimate(flops=400_000_000, bytes_accessed=2**20, transcendentals=800_000),
            name="attention",
        )(*(pltpu.with_memory_space_constraint(x, pltpu.HBM) for x in (q, k, v)))

    spec = P(("doc", "ctx"), None)
    return jax.shard_map(step, mesh=mesh, in_specs=(spec,) * 3, out_specs=spec, check_vma=False)
```

```python
import functools
import math

import jax
import jax.numpy as jnp
from jax import lax
from jax.experimental import pallas as pl
from jax.experimental.pallas import tpu as pltpu
from jax.sharding import PartitionSpec as P

MESH = pl.DeviceIdType.MESH
HEADS = 8
BOX = 128
ROWS = 8
MASKED = -1e30
TO_LOG2 = math.log2(math.e) / math.sqrt(128.0)


def pool(rows):
    count = rows.shape[0]
    target = lax.broadcasted_iota(jnp.int32, (count // 2, count), 0)
    source = lax.broadcasted_iota(jnp.int32, (count // 2, count), 1)
    pairs = jnp.where(source // 2 == target, 0.5, 0.0).astype(jnp.bfloat16)
    return jnp.dot(pairs, rows, preferred_element_type=jnp.float32).astype(jnp.bfloat16)


def attend(units):
    scores = []
    for query, keys, _, biases in units:
        parts = []
        for key, bias in zip(keys, biases):
            score = lax.dot_general(query, key, (((1,), (1,)), ((), ())), preferred_element_type=jnp.float32) * TO_LOG2
            parts.append(score if bias is None else score + bias)
        scores.append(parts)
    peaks = [jnp.max(functools.reduce(jnp.maximum, parts), axis=1, keepdims=True) for parts in scores]
    shifted = [[jnp.exp2(part - peak) for part in parts] for parts, peak in zip(scores, peaks)]
    totals = [jnp.sum(functools.reduce(jnp.add, parts), axis=1, keepdims=True) for parts in shifted]
    weights = [jnp.concatenate([part.astype(jnp.bfloat16) for part in parts], axis=1) for parts in shifted]
    numerators = [
        jnp.dot(weight, jnp.concatenate(unit[2], axis=0), preferred_element_type=jnp.float32)
        for weight, unit in zip(weights, units)
    ]
    return [
        (jnp.broadcast_to(peak, numerator.shape), jnp.broadcast_to(total, numerator.shape), numerator)
        for peak, total, numerator in zip(peaks, totals, numerators)
    ]


def merge(one, other):
    newest = jnp.maximum(one[0], other[0])
    keep_one = jnp.exp2(one[0] - newest)
    keep_other = jnp.exp2(other[0] - newest)
    return newest, one[1] * keep_one + other[1] * keep_other, one[2] * keep_one + other[2] * keep_other


def kernel(zs, q_hbm, k_hbm, v_hbm, out_ref, source, half1, far, near, relay, q1, q2, kv1, kv2, kv3, kv4, terms, ups, parcel, inbox, load_sem, send_sem, recv_sem, round_sem):
    me = lax.axis_index("ctx")
    z = me // ROWS
    rank = lax.rem(me, ROWS)
    y, core = rank // 2, lax.rem(rank, 2)
    odd = lax.rem(z, 2)

    def ring(turn, flip):
        return 2 * lax.rem(y + turn, 4) + lax.rem(core + flip, 2)

    def column(other):
        return lax.rem(other + zs, zs) * ROWS + rank

    def mate(other):
        return other + 1 - 2 * lax.rem(other, 2)

    peers = [(2, 0), (2, 1), (1, 0), (1, 1), (3, 0), (3, 1), (0, 1)]
    opposite = lax.rem(z + zs // 2, zs)
    passed_on = (z == zs // 4) | (z == zs // 4 + 1)
    mirrored = zs - 1 - z
    has_left = z > 0
    has_right = z < zs - 1
    has_a = z >= 2
    has_b = z < zs - 2
    has_c = ((odd == 0) & (z + 3 < zs)) | ((odd == 1) & (z >= 3))
    has_e = (z < 2) | (z >= zs - 2)

    loads = [
        pltpu.make_async_copy(ref, source.at[n], load_sem.at[n]) for n, ref in enumerate((k_hbm, v_hbm, q_hbm))
    ]
    for load in loads:
        load.start()

    def when(present, action):
        if present is None:
            action()
        else:
            pl.when(present)(action)

    def signal(semaphore, device):
        pl.semaphore_signal(semaphore, inc=1, device_id={"ctx": device}, device_id_type=MESH)

    barrier = pltpu.get_barrier_semaphore()
    for turn, flip in peers:
        signal(barrier, z * ROWS + ring(turn, flip))
    when(has_left, lambda: signal(barrier, column(z - 1)))
    when(has_right, lambda: signal(barrier, column(z + 1)))

    def blank(ref, present, start, count):
        @pl.when(jnp.logical_not(present))
        def _():
            ref[:, start : start + count, :] = jnp.zeros((2, count, BOX), jnp.bfloat16)

    blank(kv1, has_left, 0, 2 * BOX)
    blank(kv1, has_right, 6 * BOX, 2 * BOX)
    blank(kv2, has_left, 0, BOX)
    blank(kv2, has_right, 5 * BOX, BOX)
    blank(kv3, has_a, 0, BOX)
    blank(kv3, has_b, BOX, BOX)
    blank(kv3, has_c, 2 * BOX, BOX)
    blank(kv4, has_e, BOX, BOX)

    starts = (z == 0) & (rank == 0)
    ends = (z == zs - 1) & (rank == ROWS - 1)

    @pl.when(starts)
    def _():
        near[0] = jnp.zeros(near.shape[1:], jnp.bfloat16)

    @pl.when(ends)
    def _():
        near[1] = jnp.zeros(near.shape[1:], jnp.bfloat16)

    used = [0]
    sent = []

    def remote(src, dst, device):
        number = used[0]
        used[0] += 1
        return pltpu.make_async_remote_copy(
            src_ref=src,
            dst_ref=dst,
            send_sem=send_sem.at[number],
            recv_sem=recv_sem.at[number],
            device_id={"ctx": device},
            device_id_type=MESH,
        )

    def send(src, dst, device, goes=None, comes=None):
        copy = remote(src, dst, device)
        when(goes, copy.start)
        sent.append((copy, goes))
        return copy, comes

    def arrive(message):
        when(message[1], message[0].wait_recv)

    def head(number):
        return pl.ds(pl.multiple_of(number * BOX, BOX), BOX)

    third = BOX // 8
    for kind in range(2):
        loads[kind].wait()
        half1[kind] = pool(source[kind])
        far[kind] = pool(pool(half1[kind]))
    pl.semaphore_wait(barrier, ROWS - 1 + (z + zs - 1) // zs + (2 * zs - 2 - z) // zs)

    upward, downward, everyone = (round_sem.at[n] for n in range(3))
    when(has_left, lambda: signal(downward, column(z - 1)))

    own_third = pl.ds(pl.multiple_of(3 * BOX + rank * third, third), third)
    own_half = pl.ds(pl.multiple_of(2 * BOX + rank * (BOX // 2), BOX // 2), BOX // 2)
    own_query = pl.ds(pl.multiple_of(rank * (BOX // 2), BOX // 2), BOX // 2)
    far_in = [
        send(far.at[:, :, head(ring(turn, flip))], kv3.at[:, own_third, :], z * ROWS + ring(turn, flip))
        for turn, flip in peers
    ]
    kv_in = {
        (turn, flip): send(
            half1.at[pl.ds(0, 2), :, head(ring(turn, flip))], kv1.at[:, own_half, :], z * ROWS + ring(turn, flip)
        )
        for turn, flip in peers
    }
    loads[2].wait()
    half1[2] = pool(source[2])
    q_in = [
        send(half1.at[2, :, head(ring(turn, flip))], q1.at[own_query, :], z * ROWS + ring(turn, flip))
        for turn, flip in peers
    ]
    last = rank // (ROWS - 1)
    at_end = (rank == 0) | (rank == ROWS - 1)
    towards = (last == 1) & has_right | (rank == 0) & has_left
    behind = (last == 1) & has_left | (rank == 0) & has_right
    beyond = column(z - 1 + 2 * last)
    before = column(z + 1 - 2 * last)
    other_end = z * ROWS + ROWS - 1 - rank
    relay_keys = send(source.at[0], relay.at[0], beyond, towards, behind)

    when(has_left, lambda: pl.semaphore_wait(upward, 1))
    when(has_right, lambda: signal(upward, column(z + 1)))
    for other in range(zs // 2):
        when(z == zs - 1, lambda: signal(everyone, column(other)))

    kv3[:, own_third, :] = far[:, :, head(rank)]
    kv1[:, own_half, :] = half1[0:2, :, head(rank)]
    q1[own_query, :] = half1[2, :, head(rank)]

    near1 = []

    def send_box1(turn):
        chip = lax.rem(y + turn, 4)
        for flip in range(2):
            if ((4 - turn) % 4, flip) in kv_in:
                arrive(kv_in[(4 - turn) % 4, flip])
        up = chip >= 2
        near1.append(
            send(
                kv1.at[:, head(2 + chip), :],
                kv1.at[:, head(lax.rem(chip + 6, 8)), :],
                column(z - 1 + 2 * (chip // 2)),
                (up & has_right) | (jnp.logical_not(up) & has_left),
                (up & has_left) | (jnp.logical_not(up) & has_right),
            )
        )

    send_box1(0)
    when(has_right, lambda: pl.semaphore_wait(downward, 1))
    for message in far_in:
        arrive(message)
    own3 = kv3.at[:, pl.ds(3 * BOX, BOX), :]
    a_in = send(own3, kv3.at[:, pl.ds(0, BOX), :], column(z + 2), has_b, has_a)
    b_in = send(own3, kv3.at[:, pl.ds(BOX, BOX), :], column(z - 2), has_a, has_b)
    for kind in range(2):
        kv4[kind, 2 * BOX : 2 * BOX + BOX // 2, :] = pool(kv3[kind, 3 * BOX : 4 * BOX, :])
    own4 = kv4.at[:, pl.ds(2 * BOX, BOX // 2), :]
    half = pl.multiple_of(odd * (BOX // 2), BOX // 2)
    far4 = [
        (remote(own4, kv4.at[:, pl.ds(BOX + half, BOX // 2), :], column(mate(mirrored))), has_e),
        (remote(own4, kv4.at[:, pl.ds(BOX + half, BOX // 2), :], column(mirrored)), has_e),
        (remote(own4, kv4.at[:, pl.ds(half, BOX // 2), :], column(opposite)), z < zs - 2),
        (remote(own4, kv4.at[:, pl.ds(half, BOX // 2), :], column(mate(opposite))), z >= 0),
    ]
    sent.extend(far4)

    def send_far4(chosen):
        for copy, goes in far4:
            when(chosen & goes, copy.start)

    send_far4(z >= zs // 2)
    for turn in (1, 3, 2):
        send_box1(turn)
    for kind in range(2):
        for n in range(2):
            kv2[kind, (2 + n) * BOX : (3 + n) * BOX, :] = pool(kv1[kind, (2 * n + 2) * BOX : (2 * n + 4) * BOX, :])
    left2 = send(kv2.at[:, pl.ds(2 * BOX, BOX), :], kv2.at[:, pl.ds(0, BOX), :], column(z + 1), has_right, has_left)
    right2 = send(kv2.at[:, pl.ds(3 * BOX, BOX), :], kv2.at[:, pl.ds(5 * BOX, BOX), :], column(z - 1), has_left, has_right)

    relay_values = send(source.at[1], relay.at[1], other_end, towards, behind)
    right0 = send(source.at[pl.ds(0, 2)], near.at[0], me + 1, rank < ROWS - 1, rank > 0)
    left0 = send(source.at[pl.ds(0, 2)], near.at[1], me - 1, rank > 0, rank < ROWS - 1)

    arrive(relay_keys)
    around_keys = send(relay.at[0], near.at[1 - last, 0], other_end, behind, towards)
    arrive(a_in)
    arrive(b_in)
    c_in = send(
        kv3.at[:, head(odd), :],
        kv3.at[:, pl.ds(2 * BOX, BOX), :],
        column(mate(z)),
        ((odd == 0) & has_a) | ((odd == 1) & has_b),
        has_c,
    )

    when(z < zs // 2, lambda: pl.semaphore_wait(everyone, 1))
    send_far4(z < zs // 2)

    def bias(present):
        return jnp.where(present, 0.0, MASKED).astype(jnp.float32)

    left_bias, right_bias = bias(has_left), bias(has_right)

    arrive(relay_values)
    around_values = send(relay.at[1], near.at[last, 1], before, behind, towards)
    for message in q_in:
        arrive(message)
    for n in range(2):
        q2[n * BOX : (n + 1) * BOX, :] = pool(q1[2 * n * BOX : (2 * n + 2) * BOX, :])
    q3 = pool(q2[...])
    q4 = pool(q3)


    def box(ref, kind, start):
        return ref[kind, start * BOX : (start + 1) * BOX, :]

    def unit(query, ref, boxes, biases):
        return query, [box(ref, 0, b) for b in boxes], [box(ref, 1, b) for b in boxes], biases

    def raised(values, height):
        return values[0] + float(height), values[1], values[2]

    def repeated(values, start, times):
        count = values[0].shape[0]
        for kind in range(3):
            for turn in range(times):
                ups[kind, pl.ds(start + turn, count, times), :] = values[kind]

    def risen(start, count):
        return tuple(ups[kind, start : start + count, :] for kind in range(3))

    for message in near1:
        arrive(message)
    for kind in range(2):
        kv2[kind, BOX : 2 * BOX, :] = pool(kv1[kind, 0 : 2 * BOX, :])
        kv2[kind, 4 * BOX : 5 * BOX, :] = pool(kv1[kind, 6 * BOX : 8 * BOX, :])
    units = []
    for n, boxes in enumerate(((0, 4, 5), (1, 5, 0), (2, 6, 7), (3, 7, 2))):
        biases = [left_bias if b < 2 else right_bias if b >= 6 else None for b in boxes]
        units.append(unit(q1[n * BOX : (n + 1) * BOX, :], kv1, boxes, biases))
    level1 = [raised(values, 1) for values in attend(units)]
    arrive(far4[0])
    passed = send(
        kv4.at[:, pl.ds(pl.multiple_of(BOX + half, BOX // 2), BOX // 2), :],
        kv4.at[:, pl.ds(half, BOX // 2), :],
        column(z + 2),
        z < 2,
        passed_on,
    )

    arrive(left2)
    arrive(right2)
    units = []
    for n, boxes in enumerate(((0, 4, 5), (1, 5, 0))):
        biases = [left_bias if b < 2 else right_bias for b in boxes]
        units.append(unit(q2[n * BOX : (n + 1) * BOX, :], kv2, boxes, biases))
    for n, values in enumerate(attend(units)):
        repeated(raised(values, 2), 2 * n * BOX, 2)
        for m in range(2):
            merged = merge(level1[2 * n + m], risen((2 * n + m) * BOX, BOX))
            for kind in range(3):
                terms[kind, (2 * n + m) * BOX : (2 * n + m + 1) * BOX, :] = merged[kind]

    arrive(c_in)
    level3 = raised(attend([unit(q3, kv3, (0, 1, 2), [bias(has_a), bias(has_b), bias(has_c)])])[0], 3)
    arrive(far4[1])
    when(jnp.logical_not(passed_on), far4[2][0].wait_recv)
    arrive(passed)
    arrive(far4[3])
    repeated(raised(attend([unit(q4, kv4, (0, 1), [None, bias(has_e)])])[0], 4), 0, 2)
    repeated(merge(level3, risen(0, BOX)), 4 * BOX, 4)

    here = lax.broadcasted_iota(jnp.int32, (BOX // 2, BOX), 0) == lax.broadcasted_iota(jnp.int32, (BOX // 2, BOX), 1)
    line = lax.broadcasted_iota(jnp.int32, (16, BOX), 0)

    def finish(number, box_out):
        rows = pl.ds(pl.multiple_of(number * (BOX // 2), BOX // 2), BOX // 2)
        rows_up = pl.ds(pl.multiple_of(4 * BOX + number * (BOX // 2), BOX // 2), BOX // 2)
        peak, total, numerator = merge(
            tuple(terms[kind, rows, :] for kind in range(3)), tuple(ups[kind, rows_up, :] for kind in range(3))
        )
        box_out[0 : BOX // 2, :] = (numerator / total).astype(jnp.bfloat16)
        weight = jnp.sum(jnp.where(here, peak + jnp.log2(total), 0.0), axis=0, keepdims=True)
        high = weight.astype(jnp.bfloat16).astype(jnp.float32)
        middle = (weight - high).astype(jnp.bfloat16).astype(jnp.float32)
        parts = jnp.where(line == 0, high, jnp.where(line == 1, middle, weight - high - middle))
        box_out[BOX // 2 :, :] = jnp.where(line < 3, parts, 0.0).astype(jnp.bfloat16)

    home = {}
    for n, (turn, flip) in enumerate(peers):
        finish(ring(turn, flip), parcel.at[n])
        home[turn, flip] = send(parcel.at[n], inbox.at[rank], z * ROWS + ring(turn, flip))
    finish(rank, inbox.at[rank])

    arrive(right0)
    arrive(left0)
    arrive(around_keys)
    arrive(around_values)
    start_bias, end_bias = bias(jnp.logical_not(starts)), bias(jnp.logical_not(ends))
    for first in range(0, HEADS, 4):
        units = []
        for n in range(first, first + 4):
            columns = slice(n * BOX, (n + 1) * BOX)
            units.append(
                (
                    source[2, :, columns],
                    [near[0, 0, :, columns], source[0, :, columns], near[1, 0, :, columns]],
                    [near[0, 1, :, columns], source[1, :, columns], near[1, 1, :, columns]],
                    [start_bias, None, end_bias],
                )
            )
        for n, values in enumerate(attend(units), first):
            for kind in range(3):
                terms[kind, n * BOX : (n + 1) * BOX, :] = values[kind]

    for n, (turn, flip) in enumerate([(0, 0)] + peers[::-1]):
        if n:
            arrive(home[turn, flip])
        number = ring((4 - turn) % 4, flip)
        got = inbox.at[number]
        parts = got[BOX // 2 :, :].astype(jnp.float32)
        weight = parts[0:1, :] + parts[1:2, :] + parts[2:3, :]
        weight = jnp.sum(jnp.where(here, weight, 0.0), axis=1, keepdims=True)
        coarse = got[0 : BOX // 2, :].astype(jnp.float32)
        repeated((jnp.broadcast_to(weight, coarse.shape), jnp.ones_like(coarse), coarse), n * BOX, 2)
        fine = tuple(terms[kind, head(number), :] for kind in range(3))
        _, total, numerator = merge(fine, risen(n * BOX, BOX))
        out_ref[:, head(number)] = (numerator / total).astype(jnp.bfloat16)
    for copy, goes in sent:
        when(goes, copy.wait_send)


MESSAGES = 4 * (ROWS - 1) + 20


def solution(mesh):
    zs = mesh.shape["ctx"] // ROWS

    def step(q, k, v):
        anywhere = pl.BlockSpec(memory_space=pl.ANY)
        return pl.pallas_call(
            functools.partial(kernel, zs),
            out_shape=pltpu.VMEM(q.shape, jnp.bfloat16),
            in_specs=[anywhere] * 3,
            out_specs=pl.BlockSpec(memory_space=pltpu.VMEM),
            scratch_shapes=[
                pltpu.VMEM((3, BOX, HEADS * BOX), jnp.bfloat16),
                pltpu.VMEM((3, BOX // 2, HEADS * BOX), jnp.bfloat16),
                pltpu.VMEM((2, BOX // 8, HEADS * BOX), jnp.bfloat16),
                pltpu.VMEM((2, 2, BOX, HEADS * BOX), jnp.bfloat16),
                pltpu.VMEM((2, BOX, HEADS * BOX), jnp.bfloat16),
                pltpu.VMEM((4 * BOX, BOX), jnp.bfloat16),
                pltpu.VMEM((2 * BOX, BOX), jnp.bfloat16),
                pltpu.VMEM((2, 8 * BOX, BOX), jnp.bfloat16),
                pltpu.VMEM((2, 6 * BOX, BOX), jnp.bfloat16),
                pltpu.VMEM((2, 4 * BOX, BOX), jnp.bfloat16),
                pltpu.VMEM((2, 5 * BOX // 2, BOX), jnp.bfloat16),
                pltpu.VMEM((3, 8 * BOX, BOX), jnp.float32),
                pltpu.VMEM((3, 8 * BOX, BOX), jnp.float32),
                pltpu.VMEM((ROWS - 1, BOX // 2 + 16, BOX), jnp.bfloat16),
                pltpu.VMEM((ROWS, BOX // 2 + 16, BOX), jnp.bfloat16),
                pltpu.SemaphoreType.DMA((3,)),
                pltpu.SemaphoreType.DMA((MESSAGES,)),
                pltpu.SemaphoreType.DMA((MESSAGES,)),
                pltpu.SemaphoreType.REGULAR((3,)),
            ],
            compiler_params=pltpu.CompilerParams(
                collective_id=0, has_side_effects=True, vmem_limit_bytes=32 * 2**20
            ),
            cost_estimate=pl.CostEstimate(flops=400_000_000, bytes_accessed=2**20, transcendentals=800_000),
            name="attention",
        )(*(pltpu.with_memory_space_constraint(x, pltpu.HBM) for x in (q, k, v)))

    spec = P(("doc", "ctx"), None)
    return jax.shard_map(step, mesh=mesh, in_specs=(spec,) * 3, out_specs=spec, check_vma=False)
```

```python
import functools
import math

import jax
import jax.numpy as jnp
from jax import lax
from jax.experimental import pallas as pl
from jax.experimental.pallas import tpu as pltpu
from jax.sharding import PartitionSpec as P

MESH = pl.DeviceIdType.MESH
HEADS = 8
BOX = 128
ROWS = 8
MASKED = -1e30
TO_LOG2 = math.log2(math.e) / math.sqrt(128.0)


def pool(rows):
    count = rows.shape[0]
    target = lax.broadcasted_iota(jnp.int32, (count // 2, count), 0)
    source = lax.broadcasted_iota(jnp.int32, (count // 2, count), 1)
    pairs = jnp.where(source // 2 == target, 0.5, 0.0).astype(jnp.bfloat16)
    return jnp.dot(pairs, rows, preferred_element_type=jnp.float32).astype(jnp.bfloat16)


def attend(units):
    scores = []
    for query, keys, _, biases in units:
        parts = []
        for key, bias in zip(keys, biases):
            score = lax.dot_general(query, key, (((1,), (1,)), ((), ())), preferred_element_type=jnp.float32) * TO_LOG2
            parts.append(score if bias is None else score + bias)
        scores.append(parts)
    peaks = [jnp.max(functools.reduce(jnp.maximum, parts), axis=1, keepdims=True) for parts in scores]
    shifted = [[jnp.exp2(part - peak) for part in parts] for parts, peak in zip(scores, peaks)]
    totals = [jnp.sum(functools.reduce(jnp.add, parts), axis=1, keepdims=True) for parts in shifted]
    weights = [jnp.concatenate([part.astype(jnp.bfloat16) for part in parts], axis=1) for parts in shifted]
    numerators = [
        jnp.dot(weight, jnp.concatenate(unit[2], axis=0), preferred_element_type=jnp.float32)
        for weight, unit in zip(weights, units)
    ]
    return [
        (jnp.broadcast_to(peak, numerator.shape), jnp.broadcast_to(total, numerator.shape), numerator)
        for peak, total, numerator in zip(peaks, totals, numerators)
    ]


def merge(one, other):
    newest = jnp.maximum(one[0], other[0])
    keep_one = jnp.exp2(one[0] - newest)
    keep_other = jnp.exp2(other[0] - newest)
    return newest, one[1] * keep_one + other[1] * keep_other, one[2] * keep_one + other[2] * keep_other


def kernel(zs, q_hbm, k_hbm, v_hbm, out_ref, source, half1, far, near, relay, q1, q2, kv1, kv2, kv3, kv4, terms, ups, parcel, inbox, load_sem, send_sem, recv_sem, round_sem):
    me = lax.axis_index("ctx")
    z = me // ROWS
    rank = lax.rem(me, ROWS)
    y, core = rank // 2, lax.rem(rank, 2)
    odd = lax.rem(z, 2)

    def ring(turn, flip):
        return 2 * lax.rem(y + turn, 4) + lax.rem(core + flip, 2)

    def column(other):
        return lax.rem(other + zs, zs) * ROWS + rank

    def mate(other):
        return other + 1 - 2 * lax.rem(other, 2)

    peers = [(2, 0), (2, 1), (1, 0), (1, 1), (3, 0), (3, 1), (0, 1)]
    opposite = lax.rem(z + zs // 2, zs)
    passed_on = (z == zs // 4) | (z == zs // 4 + 1)
    mirrored = zs - 1 - z
    has_left = z > 0
    has_right = z < zs - 1
    has_a = z >= 2
    has_b = z < zs - 2
    has_c = ((odd == 0) & (z + 3 < zs)) | ((odd == 1) & (z >= 3))
    has_e = (z < 2) | (z >= zs - 2)

    loads = [
        pltpu.make_async_copy(ref, source.at[n], load_sem.at[n]) for n, ref in enumerate((k_hbm, v_hbm, q_hbm))
    ]
    for load in loads:
        load.start()

    def when(present, action):
        if present is None:
            action()
        else:
            pl.when(present)(action)

    def signal(semaphore, device):
        pl.semaphore_signal(semaphore, inc=1, device_id={"ctx": device}, device_id_type=MESH)

    barrier = pltpu.get_barrier_semaphore()
    for turn, flip in peers:
        signal(barrier, z * ROWS + ring(turn, flip))
    when(has_left, lambda: signal(barrier, column(z - 1)))
    when(has_right, lambda: signal(barrier, column(z + 1)))

    def blank(ref, present, start, count):
        @pl.when(jnp.logical_not(present))
        def _():
            ref[:, start : start + count, :] = jnp.zeros((2, count, BOX), jnp.bfloat16)

    blank(kv1, has_left, 0, 2 * BOX)
    blank(kv1, has_right, 6 * BOX, 2 * BOX)
    blank(kv2, has_left, 0, BOX)
    blank(kv2, has_right, 5 * BOX, BOX)
    blank(kv3, has_a, 0, BOX)
    blank(kv3, has_b, BOX, BOX)
    blank(kv3, has_c, 2 * BOX, BOX)
    blank(kv4, has_e, BOX, BOX)

    starts = (z == 0) & (rank == 0)
    ends = (z == zs - 1) & (rank == ROWS - 1)

    @pl.when(starts)
    def _():
        near[0] = jnp.zeros(near.shape[1:], jnp.bfloat16)

    @pl.when(ends)
    def _():
        near[1] = jnp.zeros(near.shape[1:], jnp.bfloat16)

    used = [0]
    sent = []

    def remote(src, dst, device):
        number = used[0]
        used[0] += 1
        return way(number, src, dst, device)

    def way(number, src, dst, device):
        return pltpu.make_async_remote_copy(
            src_ref=src,
            dst_ref=dst,
            send_sem=send_sem.at[number],
            recv_sem=recv_sem.at[number],
            device_id={"ctx": device},
            device_id_type=MESH,
        )

    def send(src, dst, device, goes=None, comes=None):
        copy = remote(src, dst, device)
        when(goes, copy.start)
        sent.append((copy, goes))
        return copy, comes

    def arrive(message):
        when(message[1], message[0].wait_recv)

    def head(number):
        return pl.ds(pl.multiple_of(number * BOX, BOX), BOX)

    third = BOX // 8
    for kind in range(2):
        loads[kind].wait()
        half1[kind] = pool(source[kind])
        far[kind] = pool(pool(half1[kind]))
    pl.semaphore_wait(barrier, ROWS - 1 + (z + zs - 1) // zs + (2 * zs - 2 - z) // zs)

    upward, downward, everyone = (round_sem.at[n] for n in range(3))
    when(has_left, lambda: signal(downward, column(z - 1)))

    own_third = pl.ds(pl.multiple_of(3 * BOX + rank * third, third), third)
    own_half = pl.ds(pl.multiple_of(2 * BOX + rank * (BOX // 2), BOX // 2), BOX // 2)
    own_query = pl.ds(pl.multiple_of(rank * (BOX // 2), BOX // 2), BOX // 2)
    far_in = [
        send(far.at[:, :, head(ring(turn, flip))], kv3.at[:, own_third, :], z * ROWS + ring(turn, flip))
        for turn, flip in peers
    ]
    kv_in = {
        (turn, flip): send(
            half1.at[pl.ds(0, 2), :, head(ring(turn, flip))], kv1.at[:, own_half, :], z * ROWS + ring(turn, flip)
        )
        for turn, flip in peers
    }
    loads[2].wait()
    half1[2] = pool(source[2])
    q_in = [
        send(half1.at[2, :, head(ring(turn, flip))], q1.at[own_query, :], z * ROWS + ring(turn, flip))
        for turn, flip in peers
    ]
    last = rank // (ROWS - 1)
    at_end = (rank == 0) | (rank == ROWS - 1)
    towards = (last == 1) & has_right | (rank == 0) & has_left
    behind = (last == 1) & has_left | (rank == 0) & has_right
    beyond = column(z - 1 + 2 * last)
    before = column(z + 1 - 2 * last)
    other_end = z * ROWS + ROWS - 1 - rank
    relay_keys = send(source.at[0], relay.at[0], beyond, towards, behind)

    when(has_left, lambda: pl.semaphore_wait(upward, 1))
    when(has_right, lambda: signal(upward, column(z + 1)))
    for other in range(zs // 2):
        when(z == zs - 1, lambda: signal(everyone, column(other)))

    kv3[:, own_third, :] = far[:, :, head(rank)]
    kv1[:, own_half, :] = half1[0:2, :, head(rank)]
    q1[own_query, :] = half1[2, :, head(rank)]

    near1 = []

    def send_box1(turn):
        chip = lax.rem(y + turn, 4)
        for flip in range(2):
            if ((4 - turn) % 4, flip) in kv_in:
                arrive(kv_in[(4 - turn) % 4, flip])
        up = chip >= 2
        near1.append(
            send(
                kv1.at[:, head(2 + chip), :],
                kv1.at[:, head(lax.rem(chip + 6, 8)), :],
                column(z - 1 + 2 * (chip // 2)),
                (up & has_right) | (jnp.logical_not(up) & has_left),
                (up & has_left) | (jnp.logical_not(up) & has_right),
            )
        )

    send_box1(0)
    when(has_right, lambda: pl.semaphore_wait(downward, 1))
    for message in far_in:
        arrive(message)
    own3 = kv3.at[:, pl.ds(3 * BOX, BOX), :]
    a_in = send(own3, kv3.at[:, pl.ds(0, BOX), :], column(z + 2), has_b, has_a)
    b_in = send(own3, kv3.at[:, pl.ds(BOX, BOX), :], column(z - 2), has_a, has_b)
    for kind in range(2):
        kv4[kind, 2 * BOX : 2 * BOX + BOX // 2, :] = pool(kv3[kind, 3 * BOX : 4 * BOX, :])
    own4 = kv4.at[:, pl.ds(2 * BOX, BOX // 2), :]
    half = pl.multiple_of(odd * (BOX // 2), BOX // 2)
    far4 = [
        (remote(own4, kv4.at[:, pl.ds(BOX + half, BOX // 2), :], column(mate(mirrored))), has_e),
        (remote(own4, kv4.at[:, pl.ds(BOX + half, BOX // 2), :], column(mirrored)), has_e),
        (remote(own4, kv4.at[:, pl.ds(half, BOX // 2), :], column(opposite)), z < zs - 2),
        (remote(own4, kv4.at[:, pl.ds(half, BOX // 2), :], column(mate(opposite))), z >= 0),
    ]
    sent.extend(far4)

    def send_far4(chosen):
        for copy, goes in far4:
            when(chosen & goes, copy.start)

    send_far4(z >= zs // 2)
    for turn in (1, 3, 2):
        send_box1(turn)
    for kind in range(2):
        for n in range(2):
            kv2[kind, (2 + n) * BOX : (3 + n) * BOX, :] = pool(kv1[kind, (2 * n + 2) * BOX : (2 * n + 4) * BOX, :])
    left2 = send(kv2.at[:, pl.ds(2 * BOX, BOX), :], kv2.at[:, pl.ds(0, BOX), :], column(z + 1), has_right, has_left)
    right2 = send(kv2.at[:, pl.ds(3 * BOX, BOX), :], kv2.at[:, pl.ds(5 * BOX, BOX), :], column(z - 1), has_left, has_right)

    relay_values = send(source.at[1], relay.at[1], other_end, towards, behind)
    right0 = send(source.at[pl.ds(0, 2)], near.at[0], me + 1, rank < ROWS - 1, rank > 0)
    left0 = send(source.at[pl.ds(0, 2)], near.at[1], me - 1, rank > 0, rank < ROWS - 1)

    arrive(relay_keys)
    around_keys = send(relay.at[0], near.at[1 - last, 0], other_end, behind, towards)
    arrive(a_in)
    arrive(b_in)
    c_in = send(
        kv3.at[:, head(odd), :],
        kv3.at[:, pl.ds(2 * BOX, BOX), :],
        column(mate(z)),
        ((odd == 0) & has_a) | ((odd == 1) & has_b),
        has_c,
    )

    when(z < zs // 2, lambda: pl.semaphore_wait(everyone, 1))
    send_far4(z < zs // 2)

    def bias(present):
        return jnp.where(present, 0.0, MASKED).astype(jnp.float32)

    left_bias, right_bias = bias(has_left), bias(has_right)

    arrive(relay_values)
    around_values = send(relay.at[1], near.at[last, 1], before, behind, towards)
    for message in q_in:
        arrive(message)
    for n in range(2):
        q2[n * BOX : (n + 1) * BOX, :] = pool(q1[2 * n * BOX : (2 * n + 2) * BOX, :])
    q3 = pool(q2[...])
    q4 = pool(q3)


    def box(ref, kind, start):
        return ref[kind, start * BOX : (start + 1) * BOX, :]

    def unit(query, ref, boxes, biases):
        return query, [box(ref, 0, b) for b in boxes], [box(ref, 1, b) for b in boxes], biases

    def raised(values, height):
        return values[0] + float(height), values[1], values[2]

    def repeated(values, start, times):
        count = values[0].shape[0]
        for kind in range(3):
            for turn in range(times):
                ups[kind, pl.ds(start + turn, count, times), :] = values[kind]

    def risen(start, count):
        return tuple(ups[kind, start : start + count, :] for kind in range(3))

    for message in near1:
        arrive(message)
    for kind in range(2):
        kv2[kind, BOX : 2 * BOX, :] = pool(kv1[kind, 0 : 2 * BOX, :])
        kv2[kind, 4 * BOX : 5 * BOX, :] = pool(kv1[kind, 6 * BOX : 8 * BOX, :])
    units = []
    for n, boxes in enumerate(((0, 4, 5), (1, 5, 0), (2, 6, 7), (3, 7, 2))):
        biases = [left_bias if b < 2 else right_bias if b >= 6 else None for b in boxes]
        units.append(unit(q1[n * BOX : (n + 1) * BOX, :], kv1, boxes, biases))
    level1 = [raised(values, 1) for values in attend(units)]
    arrive(far4[0])
    passed = send(
        kv4.at[:, pl.ds(pl.multiple_of(BOX + half, BOX // 2), BOX // 2), :],
        kv4.at[:, pl.ds(half, BOX // 2), :],
        column(z + 2),
        z < 2,
        passed_on,
    )

    arrive(left2)
    arrive(right2)
    units = []
    for n, boxes in enumerate(((0, 4, 5), (1, 5, 0))):
        biases = [left_bias if b < 2 else right_bias for b in boxes]
        units.append(unit(q2[n * BOX : (n + 1) * BOX, :], kv2, boxes, biases))
    for n, values in enumerate(attend(units)):
        repeated(raised(values, 2), 2 * n * BOX, 2)
        for m in range(2):
            merged = merge(level1[2 * n + m], risen((2 * n + m) * BOX, BOX))
            for kind in range(3):
                terms[kind, (2 * n + m) * BOX : (2 * n + m + 1) * BOX, :] = merged[kind]

    arrive(c_in)
    level3 = raised(attend([unit(q3, kv3, (0, 1, 2), [bias(has_a), bias(has_b), bias(has_c)])])[0], 3)
    arrive(far4[1])
    when(jnp.logical_not(passed_on), far4[2][0].wait_recv)
    arrive(passed)
    arrive(far4[3])
    repeated(raised(attend([unit(q4, kv4, (0, 1), [None, bias(has_e)])])[0], 4), 0, 2)
    repeated(merge(level3, risen(0, BOX)), 4 * BOX, 4)

    here = lax.broadcasted_iota(jnp.int32, (BOX // 2, BOX), 0) == lax.broadcasted_iota(jnp.int32, (BOX // 2, BOX), 1)
    line = lax.broadcasted_iota(jnp.int32, (16, BOX), 0)

    def finish(number, box_out):
        rows = pl.ds(pl.multiple_of(number * (BOX // 2), BOX // 2), BOX // 2)
        rows_up = pl.ds(pl.multiple_of(4 * BOX + number * (BOX // 2), BOX // 2), BOX // 2)
        peak, total, numerator = merge(
            tuple(terms[kind, rows, :] for kind in range(3)), tuple(ups[kind, rows_up, :] for kind in range(3))
        )
        box_out[0 : BOX // 2, :] = (numerator / total).astype(jnp.bfloat16)
        weight = jnp.sum(jnp.where(here, peak + jnp.log2(total), 0.0), axis=0, keepdims=True)
        high = weight.astype(jnp.bfloat16).astype(jnp.float32)
        middle = (weight - high).astype(jnp.bfloat16).astype(jnp.float32)
        parts = jnp.where(line == 0, high, jnp.where(line == 1, middle, weight - high - middle))
        box_out[BOX // 2 :, :] = jnp.where(line < 3, parts, 0.0).astype(jnp.bfloat16)

    first = used[0]
    used[0] += ROWS - 1
    for number in range(ROWS):
        turn, flip = lax.rem(number // 2 + 4 - y, 4), lax.rem(number % 2 + core, 2)
        finish(number, parcel.at[number])

        @pl.when(number != rank)
        def _():
            way(first + 2 * turn + flip - 1, parcel.at[number], inbox.at[rank], z * ROWS + number).start()

    inbox[rank] = parcel[rank]
    home = {
        (turn, flip): (way(first + 2 * turn + flip - 1, parcel.at[0], inbox.at[rank], z * ROWS + ring(turn, flip)), None)
        for turn, flip in peers
    }
    sent.extend(home.values())

    arrive(right0)
    arrive(left0)
    arrive(around_keys)
    arrive(around_values)
    start_bias, end_bias = bias(jnp.logical_not(starts)), bias(jnp.logical_not(ends))
    for first in range(0, HEADS, 4):
        units = []
        for n in range(first, first + 4):
            columns = slice(n * BOX, (n + 1) * BOX)
            units.append(
                (
                    source[2, :, columns],
                    [near[0, 0, :, columns], source[0, :, columns], near[1, 0, :, columns]],
                    [near[0, 1, :, columns], source[1, :, columns], near[1, 1, :, columns]],
                    [start_bias, None, end_bias],
                )
            )
        for n, values in enumerate(attend(units), first):
            for kind in range(3):
                terms[kind, n * BOX : (n + 1) * BOX, :] = values[kind]

    for n, (turn, flip) in enumerate([(0, 0)] + peers[::-1]):
        if n:
            arrive(home[turn, flip])
        number = ring((4 - turn) % 4, flip)
        got = inbox.at[number]
        parts = got[BOX // 2 :, :].astype(jnp.float32)
        weight = parts[0:1, :] + parts[1:2, :] + parts[2:3, :]
        weight = jnp.sum(jnp.where(here, weight, 0.0), axis=1, keepdims=True)
        coarse = got[0 : BOX // 2, :].astype(jnp.float32)
        repeated((jnp.broadcast_to(weight, coarse.shape), jnp.ones_like(coarse), coarse), n * BOX, 2)
        fine = tuple(terms[kind, head(number), :] for kind in range(3))
        _, total, numerator = merge(fine, risen(n * BOX, BOX))
        out_ref[:, head(number)] = (numerator / total).astype(jnp.bfloat16)
    for copy, goes in sent:
        when(goes, copy.wait_send)


MESSAGES = 4 * (ROWS - 1) + 20


def solution(mesh):
    zs = mesh.shape["ctx"] // ROWS

    def step(q, k, v):
        anywhere = pl.BlockSpec(memory_space=pl.ANY)
        return pl.pallas_call(
            functools.partial(kernel, zs),
            out_shape=pltpu.VMEM(q.shape, jnp.bfloat16),
            in_specs=[anywhere] * 3,
            out_specs=pl.BlockSpec(memory_space=pltpu.VMEM),
            scratch_shapes=[
                pltpu.VMEM((3, BOX, HEADS * BOX), jnp.bfloat16),
                pltpu.VMEM((3, BOX // 2, HEADS * BOX), jnp.bfloat16),
                pltpu.VMEM((2, BOX // 8, HEADS * BOX), jnp.bfloat16),
                pltpu.VMEM((2, 2, BOX, HEADS * BOX), jnp.bfloat16),
                pltpu.VMEM((2, BOX, HEADS * BOX), jnp.bfloat16),
                pltpu.VMEM((4 * BOX, BOX), jnp.bfloat16),
                pltpu.VMEM((2 * BOX, BOX), jnp.bfloat16),
                pltpu.VMEM((2, 8 * BOX, BOX), jnp.bfloat16),
                pltpu.VMEM((2, 6 * BOX, BOX), jnp.bfloat16),
                pltpu.VMEM((2, 4 * BOX, BOX), jnp.bfloat16),
                pltpu.VMEM((2, 5 * BOX // 2, BOX), jnp.bfloat16),
                pltpu.VMEM((3, 8 * BOX, BOX), jnp.float32),
                pltpu.VMEM((3, 8 * BOX, BOX), jnp.float32),
                pltpu.VMEM((ROWS, BOX // 2 + 16, BOX), jnp.bfloat16),
                pltpu.VMEM((ROWS, BOX // 2 + 16, BOX), jnp.bfloat16),
                pltpu.SemaphoreType.DMA((3,)),
                pltpu.SemaphoreType.DMA((MESSAGES,)),
                pltpu.SemaphoreType.DMA((MESSAGES,)),
                pltpu.SemaphoreType.REGULAR((3,)),
            ],
            compiler_params=pltpu.CompilerParams(
                collective_id=0, has_side_effects=True, vmem_limit_bytes=32 * 2**20
            ),
            cost_estimate=pl.CostEstimate(flops=400_000_000, bytes_accessed=2**20, transcendentals=800_000),
            name="attention",
        )(*(pltpu.with_memory_space_constraint(x, pltpu.HBM) for x in (q, k, v)))

    spec = P(("doc", "ctx"), None)
    return jax.shard_map(step, mesh=mesh, in_specs=(spec,) * 3, out_specs=spec, check_vma=False)
```
